32 devices in a mesh: groups: 2 (over x), blk: 8 (over z, y), dim: 2 (over core).
Axes of the slice: x: 2, y: 2, z: 4, core: 2. Of those that a mesh axis runs over, the one named last changes fastest.
Arguments:
- gradients: bfloat16 [4096, 128, 128], P(('groups', 'blk'), 'dim'), parts along dimension 0, may hold values from -60 to 60
- owner_of: int32 [4096, 1], P(('groups', 'blk')), parts along dimension 0, may hold values from 0 to 7; in each aligned block of 256 rows (0 to 255, 256 to 511, ...) at most 48 rows name the same one
- pair_flags: int32 [16, 3], P('groups'), parts along dimension 0, may hold values from 0 to 1, as said below
- left_factor: bfloat16 [128, 128], replicated, may hold values from -0.5 to 0.5
- right_factor: bfloat16 [128, 128], replicated, may hold values from -0.5 to 0.5
Outputs:
- tiles: bfloat16 [96, 384, 384], P(('groups', 'blk'), None, 'dim'), parts along dimension 0
- self_influence: bfloat16 [6144], P(('groups', 'blk')), parts along dimension 0
The draws below stay inside these ranges and needn't reach their ends.
There are 2 independent parts, one for each index of `groups`. The reference program is written for one: setup_inputs(seed, part) draws one part's arguments, and reference() takes and returns one part's arrays. A program takes and returns all parts, laid end to end along the dimension named above; an argument that names none is the same for every part. Nothing has to cross between parts.
Inputs may be any that keep to these rules, and one draw needn't show every extreme that they name: `owner_of`: at most 48 of the 256 examples of one producer name the same owner. `pair_flags`: 1 where block a is compared with block (a + j + 1) mod 8, else 0.
All inputs are finite; a program needn't handle non-finite values.
Results may differ from the reference program's by a relative error of at most 0.0031.
The reference program's roundings to bfloat16 on the way (of `normed`, `influence` and `cluster`) count: a program that leaves them out, or rounds other values in their place, can miss the bound.
Values may be sent and summed in bfloat16 or wider, within the bound.
No kernel may reach another device: no remote copies, remote signals or barrier semaphores. Data moves between devices by JAX's collectives and lax.ppermute only.
A program may use at most 128 MiB of HBM per device.

```python
import math
import jax
import jax.numpy as jnp
import numpy as np
from jax import lax

FACT = 128
EX_DEV = 256
REACH = 3
SLOT = 48
BLOCK = 384
EXAMPLES = 2048
N_BLK = 8


def draw_gradients(key, part):
    key = jax.random.fold_in(key, 11)
    first, second = jax.random.split(key, 2)
    shape = (EXAMPLES, FACT, FACT)
    scales = jnp.exp(jax.random.uniform(second, (EXAMPLES, 1, 1), jnp.float32, 0.0, math.log(10.0)))
    values = jnp.clip(jax.random.normal(first, shape, jnp.float32), -4.0, 4.0) * scales
    return values.astype(jnp.bfloat16)


def draw_pair_flags(key, part):
    key = jax.random.fold_in(key, 23)
    first, second = jax.random.split(key, 2)
    level = jax.random.randint(first, (N_BLK, 1), 1, 5)
    values = jax.random.randint(second, (N_BLK, REACH), 0, 4)
    return (values < level).astype(jnp.int32)


def shared_out(own_key, own, number, rows, number_of, top, limit, lean):
    order = jax.random.permutation(own_key, number_of)
    crowded, usual = shares(number_of, rows * top, limit, lean, True), shares(number_of, rows * top, limit, lean, False)
    places = jnp.arange(number_of)

    def named(lengths, offset_by):
        used = int((lengths > 0).sum())
        fixed = max(1, used // 4)
        passed = fixed + (places - fixed + offset_by * (used - fixed)) % max(1, number_of - fixed)
        return jnp.zeros((number_of,), jnp.int32).at[order[jnp.where(places < fixed, places, passed)]].set(jnp.asarray(lengths, jnp.int32))

    lengths = jnp.where(number % 4 == 0, named(crowded, number // 4), named(usual, number - number // 4 - 1))
    mixed = jax.random.permutation(jax.random.fold_in(own, 3), number_of)
    giver, taker = mixed[0:number_of // 2 * 2:2], mixed[1:number_of // 2 * 2:2]
    margin = jnp.minimum(lengths[giver] - 1, limit - lengths[taker]) // 2
    margin = jnp.where((giver == order[0]) | (taker == order[0]) | (lengths[taker] == 0), 0, jnp.maximum(margin, 0))
    passed = jax.random.randint(jax.random.fold_in(own, 4), (number_of // 2,), 0, 1 << 20) % (margin + 1)
    lengths = lengths.at[giver].add(-passed).at[taker].add(passed)
    members = jnp.searchsorted(jnp.cumsum(lengths), jnp.arange(rows * top), side="right").astype(jnp.int32)
    listing = members.reshape(top, rows).T
    listing = listing[jax.random.permutation(jax.random.fold_in(own, 1), rows)]
    offset_by = jax.random.randint(jax.random.fold_in(own, 2), (rows, 1), 0, top)
    return jnp.take_along_axis(listing, (jnp.arange(top)[None, :] + offset_by) % top, axis=1)


def shares(amount, total, bound, slope, full):
    weights = [(1 << 20) // math.isqrt(grade ** slope) + 1 for grade in range(1, amount + 1)]
    largest = bound if full else min(bound, max(-(-total // amount), total * weights[0] // sum(weights)))
    least = 1 if total - largest >= amount - 1 else 0
    counts, surplus = [largest] + [least] * (amount - 1), total - largest - least * (amount - 1)
    while surplus > 0:
        candidates = [i for i in range(1, amount) if counts[i] < largest] or [i for i in range(1, amount) if counts[i] < bound]
        pool, remaining = sum([weights[i] for i in candidates]), surplus
        for i in candidates:
            extra = min(bound - counts[i], max(1, remaining * weights[i] // pool), surplus)
            counts[i] = counts[i] + extra
            surplus = surplus - extra
    return np.array(counts)


def normal_values(rng, shape, spread, most, kind=jnp.bfloat16):
    array = jax.random.normal(rng, shape, jnp.float32) * spread
    return jnp.minimum(jnp.maximum(array, -most), most).astype(kind)


def setup_inputs(seed: int = 0, part: int = 0) -> dict:
    splits = jax.random.split(jax.random.key(seed), 6)
    own_keys = jax.random.split(jax.random.fold_in(splits[5], part), 6)
    gradients = draw_gradients(jax.random.fold_in(jax.random.fold_in(splits[5], part), 71), part)
    owner_of_keys = jax.random.split(jax.random.fold_in(own_keys[1], 1), EXAMPLES // EX_DEV)
    owner_of_turns = jax.random.permutation(jax.random.fold_in(own_keys[1], 3), EXAMPLES // EX_DEV)
    owner_of = jax.vmap(lambda own, number: shared_out(jax.random.fold_in(own_keys[1], 2), own, number, EX_DEV, N_BLK, 1, SLOT, 2))(owner_of_keys, owner_of_turns).reshape((EXAMPLES, 1))
    pair_flags = draw_pair_flags(jax.random.fold_in(jax.random.fold_in(splits[5], part), 71), part)
    left_factor = normal_values(splits[3], (FACT, FACT), FACT ** -0.5, 0.5)
    right_factor = normal_values(splits[4], (FACT, FACT), FACT ** -0.5, 0.5)
    return {"gradients": gradients, "owner_of": owner_of, "pair_flags": pair_flags, "left_factor": left_factor, "right_factor": right_factor}


def precondition(block, left_factor, right_factor):
    highest = lax.Precision.HIGHEST
    left = jnp.einsum('ik,ekc->eic', left_factor.astype(jnp.float32), block.astype(jnp.float32), precision=highest)
    return jnp.einsum('eic,cd->eid', left, right_factor.astype(jnp.float32), precision=highest)

def reference(gradients, owner_of, pair_flags, left_factor, right_factor):
    feat = FACT * FACT

    def produce(block):
        full = precondition(block, left_factor, right_factor)
        mean_sq = lax.optimization_barrier(jnp.sum(full * full, axis=(1, 2))) / feat
        normed = (full * lax.rsqrt(mean_sq + 1e-06)[:, None, None]).astype(jnp.bfloat16)
        influence = jnp.log1p(mean_sq).astype(jnp.bfloat16)
        return (normed.reshape(EX_DEV, feat), influence)
    normed, influence = lax.map(produce, gradients.reshape(N_BLK, EX_DEV, FACT, FACT))
    owners = owner_of[:, 0].reshape(N_BLK, EX_DEV)
    onehot = (owners[:, :, None] == jnp.arange(N_BLK, dtype=jnp.int32)[None, None, :]).astype(jnp.int32)
    earlier = jnp.cumsum(onehot, axis=1) - onehot
    rank = lax.optimization_barrier(jnp.sum(earlier * onehot, axis=2))
    target = owners * BLOCK + jnp.arange(N_BLK, dtype=jnp.int32)[:, None] * SLOT + rank
    target = target.reshape(-1).astype(jnp.int32)
    cluster = jnp.zeros((N_BLK * BLOCK, feat), jnp.bfloat16).at[target].set(normed.reshape(-1, feat))
    self_influence = jnp.zeros((N_BLK * BLOCK,), jnp.bfloat16).at[target].set(influence.reshape(-1))
    cluster = cluster.reshape(N_BLK, BLOCK, feat)
    scale = feat ** (-0.5)
    flags = pair_flags.astype(jnp.float32)

    def forward(index):
        own = lax.dynamic_index_in_dim(cluster, index, 0, keepdims=False)
        result = []
        for step in range(REACH):
            other_index = ((index + step + 1) % N_BLK).astype(jnp.int32)
            other = lax.dynamic_index_in_dim(cluster, other_index, 0, keepdims=False)
            product = jnp.dot(own, other.T, preferred_element_type=jnp.float32)
            weight = lax.dynamic_index_in_dim(flags, index, 0, keepdims=False)[step]
            result.append(product * (weight * scale))
        return jnp.stack(result).astype(jnp.bfloat16)
    fwd = lax.map(forward, jnp.arange(N_BLK, dtype=jnp.int32))
    back = jnp.stack([jnp.roll(fwd[:, step], step + 1, axis=0).transpose(0, 2, 1) for step in range(REACH)], axis=1)
    tiles = jnp.concatenate([fwd, back], axis=1).reshape(N_BLK * 2 * REACH, BLOCK, BLOCK)
    return (tiles, self_influence)
```

```python
import functools

import jax
import jax.numpy as jnp
from jax import lax
from jax.experimental import pallas as pl
from jax.experimental.pallas import tpu as pltpu
from jax.sharding import PartitionSpec as P

PARTIAL_BYTES = 16 * 2**20
CHUNKS = (1, 1, 1, 1)
GROUP = 8
STEP = 32
VMEM_BYTES = 56 * 2**20


def from_behind(shard, axis, by):
    peers = lax.axis_size(axis)
    return lax.ppermute(shard, axis, [(i, (i + by) % peers) for i in range(peers)])


def slot_targets(owner_of, owners_count, slots):
    owners = owner_of[:, 0]
    onehot = (owners[:, None] == jnp.arange(owners_count, dtype=jnp.int32)[None, :]).astype(
        jnp.int32
    )
    earlier = jnp.cumsum(onehot, axis=0) - onehot
    rank = jnp.sum(earlier * onehot, axis=1)
    return owners * slots + rank


def ring_plan(gradients, owner_of, pair_flags, left_factor, right_factor):
    count, half, width = gradients.shape
    halves = lax.axis_size("dim")
    position = lax.axis_index("dim")
    feat = half * width * halves
    highest = lax.Precision.HIGHEST
    whole = lax.all_gather(gradients, "dim", axis=1, tiled=True)
    left_rows = lax.dynamic_slice_in_dim(left_factor, position * half, half, 0)
    left_side = jnp.einsum("ik,ekc->eic", left_rows, whole, preferred_element_type=jnp.float32)
    full = jnp.einsum("eic,cd->eid", left_side, right_factor.astype(jnp.float32), precision=highest)
    mean_sq = lax.psum(jnp.sum(full * full, axis=(1, 2)), "dim") / feat
    normed = (
        (full * lax.rsqrt(mean_sq + 1e-06)[:, None, None])
        .astype(jnp.bfloat16)
        .reshape(count, half * width)
    )
    influence = jnp.log1p(mean_sq).astype(jnp.bfloat16)
    owners_count = lax.axis_size("blk")
    slots = 3 * count // (2 * owners_count)
    block = owners_count * slots
    target = slot_targets(owner_of, owners_count, slots)
    placing = (jnp.arange(block, dtype=jnp.int32)[:, None] == target[None, :]).astype(jnp.bfloat16)
    outgoing = jnp.dot(placing, normed, preferred_element_type=jnp.float32).astype(jnp.bfloat16)
    outgoing = outgoing.reshape(owners_count, slots, half * width)
    sent_influence = jnp.dot(placing, influence, preferred_element_type=jnp.float32).astype(
        jnp.bfloat16
    )
    sent_influence = sent_influence.reshape(owners_count, slots)
    received, got_influence = (
        lax.all_to_all(outgoing, "blk", split_axis=0, concat_axis=0, tiled=True),
        lax.all_to_all(sent_influence, "blk", split_axis=0, concat_axis=0, tiled=True),
    )
    own = received.reshape(block, half * width)
    self_influence = got_influence.reshape(block)
    reach = pair_flags.shape[1]
    owner_index = lax.axis_index("blk")
    picker = (jnp.arange(owners_count, dtype=jnp.int32) == owner_index).astype(jnp.float32)
    flags = pair_flags.astype(jnp.float32)
    ahead_flags = jnp.dot(picker, flags)
    scale = feat ** (-0.5)
    partials = []
    for step in range(1, reach + 1):
        ahead = from_behind(own, "blk", -step)
        product = jnp.dot(own, ahead.T, preferred_element_type=jnp.float32)
        partials.append(product * (ahead_flags[step - 1] * scale))
    partials = partials + [term.T for term in partials]
    summed = lax.psum_scatter(jnp.stack(partials), "dim", scatter_dimension=2, tiled=True).astype(
        jnp.bfloat16
    )
    returned = [from_behind(summed[reach + step - 1], "blk", step) for step in range(1, reach + 1)]
    summed = jnp.concatenate([summed[:reach], jnp.stack(returned)], axis=0)
    return (summed, self_influence)


def precondition_kernel(rows, spot, own, other, left, right, *rest):
    outs, mean_sq, full, sums, parts = rest[:-4], rest[-4], rest[-3], rest[-2], rest[-1]
    here = spot[0]
    batch, half, width = own.shape
    side = 2 * half
    for first in range(0, batch, GROUP):
        for e in range(first, first + GROUP, 2):
            pair = [jnp.concatenate([own[i], other[i]], axis=0) for i in (e, e + 1)]
            sides = jnp.dot(
                left[...], jnp.concatenate(pair, axis=1), preferred_element_type=jnp.float32
            )
            for i in range(2):
                term = sides[:, i * width : (i + 1) * width]
                high = term.astype(jnp.bfloat16)
                term = term - high.astype(jnp.float32)
                mid = term.astype(jnp.bfloat16)
                low = (term - mid.astype(jnp.float32)).astype(jnp.bfloat16)
                parts[pl.ds((e - first + i) * side, side), :] = jnp.concatenate(
                    [high, mid, low], axis=1
                )
        product = jnp.dot(parts[...], right[...], preferred_element_type=jnp.float32)
        full[pl.ds(first * side, GROUP * side), :] = product
        squares = (product * product).reshape(GROUP, side // 8, 8, width)
        sums[pl.ds(first * 8, GROUP * 8), :] = jnp.sum(squares, axis=1).reshape(GROUP * 8, width)
    total = sums[pl.ds(0, batch, stride=8), :]
    for s in range(1, 8):
        total = total + sums[pl.ds(s, batch, stride=8), :]
    mean = jnp.sum(total, axis=1, keepdims=True) / (side * width)
    mean_sq[...] = jnp.broadcast_to(mean, (batch, width))
    scale = jnp.broadcast_to(lax.rsqrt(mean + 1e-06), (batch, width))
    for k in range(len(outs)):
        base = lax.bitwise_xor(here, k) * rows
        for r in range(rows):
            values = full[pl.ds(base + r, batch, stride=side), :]
            outs[k][:, r * width : (r + 1) * width] = (values * scale).astype(jnp.bfloat16)


def precondition(spot, own, other, left, right, quads):
    count, half, width = own.shape
    side = 2 * half
    rows = half // quads
    batch = min(STEP, count)
    gradient_spec = pl.BlockSpec((batch, half, width), lambda i, s: (i, 0, 0))
    return pl.pallas_call(
        functools.partial(precondition_kernel, rows),
        grid_spec=pltpu.PrefetchScalarGridSpec(
            num_scalar_prefetch=1,
            grid=(count // batch,),
            in_specs=[
                gradient_spec,
                gradient_spec,
                pl.BlockSpec((side, side), lambda i, s: (0, 0)),
                pl.BlockSpec((3 * width, width), lambda i, s: (0, 0)),
            ],
            out_specs=[pl.BlockSpec((batch, rows * width), lambda i, s: (i, 0))] * quads
            + [pl.BlockSpec((batch, width), lambda i, s: (i, 0))],
            scratch_shapes=[
                pltpu.VMEM((batch * side, width), jnp.float32),
                pltpu.VMEM((batch * 8, width), jnp.float32),
                pltpu.VMEM((GROUP * side, 3 * width), jnp.bfloat16),
            ],
        ),
        out_shape=[jax.ShapeDtypeStruct((count, rows * width), jnp.bfloat16)] * quads
        + [jax.ShapeDtypeStruct((count, width), jnp.float32)],
        compiler_params=pltpu.CompilerParams(vmem_limit_bytes=VMEM_BYTES),
        cost_estimate=pl.CostEstimate(
            flops=2 * count * side * side * width * 4,
            bytes_accessed=count * half * width * 6,
            transcendentals=0,
        ),
        name="precondition",
    )(spot, own, other, left, right)


def tiles_kernel(quads, reach, slots, spot, targets, *rest):
    owners = 2 * quads
    outs = quads * reach * 2
    inputs, sums, (cluster,) = rest[: -outs - 1], rest[-outs - 1 : -1], rest[-1:]
    pieces = len(inputs) // owners
    here, side, core = spot[0], spot[1], spot[2]
    block = owners * slots
    count = targets.shape[2]
    depth = inputs[0].shape[1]

    @pl.when(pl.program_id(0) == 0)
    def _():
        for ref in sums:
            ref[...] = jnp.zeros_like(ref)

    slot_of = lax.broadcasted_iota(jnp.int32, (block, count), 0)
    for source in range(owners):
        k, m = source % quads, source // quads
        producer = 2 * lax.bitwise_xor(here, k) + lax.bitwise_xor(side, m)
        placing = (slot_of == targets[producer]).astype(jnp.bfloat16)
        values = jnp.concatenate([r[...] for r in inputs[source * pieces : (source + 1) * pieces]])
        placed = jnp.dot(placing, values, preferred_element_type=jnp.float32).astype(jnp.bfloat16)
        cluster[:, producer] = placed.reshape(owners, slots, depth)
    for k in range(quads):
        owner = 2 * lax.bitwise_xor(here, k) + side
        mine = cluster[owner].reshape(block, depth)
        for j in range(reach):
            ahead = cluster[lax.rem(owner + j + 1, owners)].reshape(block, depth)
            product = lax.dot_general(
                ahead, mine, (((1,), (1,)), ((), ())), preferred_element_type=jnp.float32
            )
            keep, send = sums[2 * (k * reach + j)], sums[2 * (k * reach + j) + 1]

            @pl.when(core == 0)
            def _():
                keep[...] += product[: block // 2]
                send[...] += product[block // 2 :]

            @pl.when(core != 0)
            def _():
                send[...] += product[: block // 2]
                keep[...] += product[block // 2 :]


def partial_tiles(spot, targets, pieces, quads, reach, slots):
    owners = 2 * quads
    block = owners * slots
    count = targets.shape[2]
    features = pieces[0].shape[1]
    depth = min(512, features)
    in_specs = [pl.BlockSpec(targets.shape, lambda i, s: (0, 0, 0))]
    in_specs += [pl.BlockSpec((p.shape[0], depth), lambda i, s: (0, i)) for p in pieces]
    outs = quads * reach * 2
    return pl.pallas_call(
        functools.partial(tiles_kernel, quads, reach, slots),
        grid_spec=pltpu.PrefetchScalarGridSpec(
            num_scalar_prefetch=1,
            grid=(features // depth,),
            in_specs=in_specs,
            out_specs=[pl.BlockSpec((block // 2, block), lambda i, s: (0, 0))] * outs,
            scratch_shapes=[pltpu.VMEM((owners, owners, slots, depth), jnp.bfloat16)],
        ),
        out_shape=[jax.ShapeDtypeStruct((block // 2, block), jnp.float32)] * outs,
        compiler_params=pltpu.CompilerParams(vmem_limit_bytes=VMEM_BYTES),
        cost_estimate=pl.CostEstimate(
            flops=2 * features * block * (owners * count + quads * reach * block),
            bytes_accessed=owners * count * features * 2 + outs * block * block * 2,
            transcendentals=0,
        ),
        name="partial_tiles",
    )(spot, targets, *pieces)


def split_plan(gradients, owner_of, pair_flags, left_factor, right_factor):
    count, half, width = gradients.shape
    feat = 2 * half * width
    owners = lax.axis_size("blk")
    quads = owners // 2
    reach = pair_flags.shape[1]
    slots = 3 * count // (2 * owners)
    block = owners * slots
    index = lax.axis_index("blk")
    core = lax.axis_index("dim")
    here, side = index // 2, index % 2
    spot = jnp.stack([here, side, core]).astype(jnp.int32)

    def across(x):
        return lax.ppermute(x, "dim", [(0, 1), (1, 0)])

    def along(x, k):
        return lax.ppermute(x, "blk", [(i, i ^ (2 * k)) for i in range(owners)])

    def beside(x):
        return lax.ppermute(x, "blk", [(i, i ^ 1) for i in range(owners)])

    swapped = jnp.concatenate([left_factor[half:], left_factor[:half]], axis=0)
    swapped = jnp.concatenate([swapped[:, half:], swapped[:, :half]], axis=1)
    left = jnp.where(core == 0, left_factor, swapped)
    right = jnp.concatenate([right_factor] * 3, axis=0)

    target = slot_targets(owner_of, owners, slots)
    targets = lax.all_gather(target, "blk", axis=0, tiled=True).reshape(owners, 1, count)

    bounds = [0]
    for part in CHUNKS:
        bounds.append(bounds[-1] + part * count // sum(CHUNKS))
    chunks = [gradients[a:b] for a, b in zip(bounds[:-1], bounds[1:])]
    others = [across(chunk) for chunk in chunks]
    pieces = [[] for _ in range(owners)]
    means = []
    for chunk, other in zip(chunks, others):
        *parts, mean_sq = precondition(spot, chunk, other, left, right, quads)
        means.append(mean_sq[:, 0])
        got = [parts[0]] + [None] * (quads - 1)
        for k in reversed(range(1, quads)):
            got[k] = along(parts[k], k)
        for k in range(quads):
            pieces[k].append(got[k])
            pieces[quads + k].append(beside(got[k]))

    influence = jnp.log1p(jnp.concatenate(means)).astype(jnp.bfloat16)
    influences = lax.all_gather(influence, "blk", axis=0, tiled=True).reshape(owners, count)
    local = targets[:, 0] - index * slots
    chosen = local[:, None, :] == jnp.arange(slots, dtype=jnp.int32)[None, :, None]
    self_influence = jnp.sum(
        jnp.where(chosen, influences[:, None, :].astype(jnp.float32), 0.0), axis=2
    ).astype(jnp.bfloat16)

    sums = partial_tiles(
        spot, targets, [p for group in pieces for p in group], quads, reach, slots
    )
    flags = lax.dynamic_index_in_dim(pair_flags, index, 0, keepdims=False).astype(jnp.float32)
    ahead, behind = [], []
    for j in range(reach):
        total = [None] * quads
        for k in reversed(range(quads)):
            at = 2 * (k * reach + j)
            total[k] = sums[at] + across(sums[at + 1])
        bit = 1
        while bit < quads:
            for k in range(0, quads, 2 * bit):
                total[k] = total[k] + along(total[k + bit], bit)
            bit *= 2
        tile = (total[0] * (flags[j] * feat ** (-0.5))).astype(jnp.bfloat16)
        ahead.append(tile)
        turned = tile.T.reshape(2, block // 2, block // 2)
        straight = lax.dynamic_index_in_dim(turned, core, 0, keepdims=False)
        crossed = lax.dynamic_index_in_dim(turned, 1 - core, 0, keepdims=False)
        by = j + 1
        straight = from_behind(straight, "blk", by)
        crossed = lax.ppermute(
            crossed,
            ("blk", "dim"),
            [(2 * i + c, 2 * ((i + by) % owners) + 1 - c) for i in range(owners) for c in range(2)],
        )
        behind.append(
            jnp.where(
                core == 0,
                jnp.concatenate([straight, crossed], axis=1),
                jnp.concatenate([crossed, straight], axis=1),
            )
        )
    tiles = jnp.stack(ahead + behind).swapaxes(1, 2)
    return (tiles, self_influence.reshape(block))


def solution(mesh):
    owners = mesh.shape["blk"]

    def per_device(gradients, owner_of, pair_flags, left_factor, right_factor):
        block = 3 * gradients.shape[0] // 2
        partial_bytes = 4 * owners * pair_flags.shape[1] * block * block // 2
        quads = owners // 2
        fits = partial_bytes <= PARTIAL_BYTES and quads & (quads - 1) == 0
        plan = split_plan if fits and gradients.shape[1] % quads == 0 else ring_plan
        return plan(gradients, owner_of, pair_flags, left_factor, right_factor)

    return jax.shard_map(
        per_device,
        mesh=mesh,
        in_specs=(
            P(("groups", "blk"), "dim", None),
            P(("groups", "blk"), None),
            P("groups", None),
            P(),
            P(),
        ),
        out_specs=(P(("groups", "blk"), None, "dim"), P(("groups", "blk"))),
        check_vma=False,
    )
```

```python
import functools

import jax
import jax.numpy as jnp
from jax import lax
from jax.experimental import pallas as pl
from jax.experimental.pallas import tpu as pltpu
from jax.sharding import PartitionSpec as P

PARTIAL_BYTES = 16 * 2**20
FIRST = 64
SLICES = (3, 3, 2)
PLACE_WIDTH = 256
GROUP = 8
STEP = 32
VMEM_BYTES = 56 * 2**20


def from_behind(shard, axis, by):
    peers = lax.axis_size(axis)
    return lax.ppermute(shard, axis, [(i, (i + by) % peers) for i in range(peers)])


def slot_targets(owner_of, owners_count, slots):
    owners = owner_of[:, 0]
    onehot = (owners[:, None] == jnp.arange(owners_count, dtype=jnp.int32)[None, :]).astype(
        jnp.int32
    )
    earlier = jnp.cumsum(onehot, axis=0) - onehot
    rank = jnp.sum(earlier * onehot, axis=1)
    return owners * slots + rank


def ring_plan(gradients, owner_of, pair_flags, left_factor, right_factor):
    count, half, width = gradients.shape
    halves = lax.axis_size("dim")
    position = lax.axis_index("dim")
    feat = half * width * halves
    highest = lax.Precision.HIGHEST
    whole = lax.all_gather(gradients, "dim", axis=1, tiled=True)
    left_rows = lax.dynamic_slice_in_dim(left_factor, position * half, half, 0)
    left_side = jnp.einsum("ik,ekc->eic", left_rows, whole, preferred_element_type=jnp.float32)
    full = jnp.einsum("eic,cd->eid", left_side, right_factor.astype(jnp.float32), precision=highest)
    mean_sq = lax.psum(jnp.sum(full * full, axis=(1, 2)), "dim") / feat
    normed = (
        (full * lax.rsqrt(mean_sq + 1e-06)[:, None, None])
        .astype(jnp.bfloat16)
        .reshape(count, half * width)
    )
    influence = jnp.log1p(mean_sq).astype(jnp.bfloat16)
    owners_count = lax.axis_size("blk")
    slots = 3 * count // (2 * owners_count)
    block = owners_count * slots
    target = slot_targets(owner_of, owners_count, slots)
    placing = (jnp.arange(block, dtype=jnp.int32)[:, None] == target[None, :]).astype(jnp.bfloat16)
    outgoing = jnp.dot(placing, normed, preferred_element_type=jnp.float32).astype(jnp.bfloat16)
    outgoing = outgoing.reshape(owners_count, slots, half * width)
    sent_influence = jnp.dot(placing, influence, preferred_element_type=jnp.float32).astype(
        jnp.bfloat16
    )
    sent_influence = sent_influence.reshape(owners_count, slots)
    received, got_influence = (
        lax.all_to_all(outgoing, "blk", split_axis=0, concat_axis=0, tiled=True),
        lax.all_to_all(sent_influence, "blk", split_axis=0, concat_axis=0, tiled=True),
    )
    own = received.reshape(block, half * width)
    self_influence = got_influence.reshape(block)
    reach = pair_flags.shape[1]
    owner_index = lax.axis_index("blk")
    picker = (jnp.arange(owners_count, dtype=jnp.int32) == owner_index).astype(jnp.float32)
    flags = pair_flags.astype(jnp.float32)
    ahead_flags = jnp.dot(picker, flags)
    scale = feat ** (-0.5)
    partials = []
    for step in range(1, reach + 1):
        ahead = from_behind(own, "blk", -step)
        product = jnp.dot(own, ahead.T, preferred_element_type=jnp.float32)
        partials.append(product * (ahead_flags[step - 1] * scale))
    partials = partials + [term.T for term in partials]
    summed = lax.psum_scatter(jnp.stack(partials), "dim", scatter_dimension=2, tiled=True).astype(
        jnp.bfloat16
    )
    returned = [from_behind(summed[reach + step - 1], "blk", step) for step in range(1, reach + 1)]
    summed = jnp.concatenate([summed[:reach], jnp.stack(returned)], axis=0)
    return (summed, self_influence)


def after(values, *deps):
    return list(lax.optimization_barrier((tuple(values), deps))[0])


def precondition_kernel(widths, spot, own, other, left, right, *rest):
    quads = len(rest[:-4]) // len(widths)
    outs, mean_sq, full, sums, parts = rest[:-4], rest[-4], rest[-3], rest[-2], rest[-1]
    here = spot[0]
    batch, half, width = own.shape
    side = 2 * half
    for first in range(0, batch, GROUP):
        for e in range(first, first + GROUP, 2):
            pair = [jnp.concatenate([own[i], other[i]], axis=0) for i in (e, e + 1)]
            sides = jnp.dot(
                left[...], jnp.concatenate(pair, axis=1), preferred_element_type=jnp.float32
            )
            for i in range(2):
                term = sides[:, i * width : (i + 1) * width]
                high = term.astype(jnp.bfloat16)
                term = term - high.astype(jnp.float32)
                mid = term.astype(jnp.bfloat16)
                low = (term - mid.astype(jnp.float32)).astype(jnp.bfloat16)
                parts[pl.ds((e - first + i) * side, side), :] = jnp.concatenate(
                    [high, mid, low], axis=1
                )
        product = jnp.dot(parts[...], right[...], preferred_element_type=jnp.float32)
        full[pl.ds(first * side, GROUP * side), :] = product
        squares = (product * product).reshape(GROUP, side // 8, 8, width)
        sums[pl.ds(first * 8, GROUP * 8), :] = jnp.sum(squares, axis=1).reshape(GROUP * 8, width)
    total = sums[pl.ds(0, batch, stride=8), :]
    for s in range(1, 8):
        total = total + sums[pl.ds(s, batch, stride=8), :]
    mean = jnp.sum(total, axis=1, keepdims=True) / (side * width)
    mean_sq[...] = jnp.broadcast_to(mean, (batch, width))
    scale = jnp.broadcast_to(lax.rsqrt(mean + 1e-06), (batch, width))
    for k in range(quads):
        base = lax.bitwise_xor(here, k) * (half // quads)
        row = 0
        for f, wide in enumerate(widths):
            out = outs[k * len(widths) + f]
            for r in range(wide // width):
                values = full[pl.ds(base + row, batch, stride=side), :]
                out[:, r * width : (r + 1) * width] = (values * scale).astype(jnp.bfloat16)
                row += 1


def precondition(spot, own, other, left, right, span, widths, quads):
    _, half, width = own.shape
    side = 2 * half
    first, count, batch = span
    gradient_spec = pl.BlockSpec((batch, half, width), lambda i, s: (first // batch + i, 0, 0))
    widths_all = list(widths) * quads
    return pl.pallas_call(
        functools.partial(precondition_kernel, widths),
        grid_spec=pltpu.PrefetchScalarGridSpec(
            num_scalar_prefetch=1,
            grid=(count // batch,),
            in_specs=[
                gradient_spec,
                gradient_spec,
                pl.BlockSpec((side, side), lambda i, s: (0, 0)),
                pl.BlockSpec((3 * width, width), lambda i, s: (0, 0)),
            ],
            out_specs=[
                pl.BlockSpec((batch, wide), lambda i, s: (i, 0)) for wide in widths_all
            ]
            + [pl.BlockSpec((batch, width), lambda i, s: (i, 0))],
            scratch_shapes=[
                pltpu.VMEM((batch * side, width), jnp.float32),
                pltpu.VMEM((batch * 8, width), jnp.float32),
                pltpu.VMEM((GROUP * side, 3 * width), jnp.bfloat16),
            ],
        ),
        out_shape=[jax.ShapeDtypeStruct((count, wide), jnp.bfloat16) for wide in widths_all]
        + [jax.ShapeDtypeStruct((count, width), jnp.float32)],
        compiler_params=pltpu.CompilerParams(vmem_limit_bytes=VMEM_BYTES),
        cost_estimate=pl.CostEstimate(
            flops=2 * count * side * side * width * 4,
            bytes_accessed=count * half * width * 6,
            transcendentals=0,
        ),
        name="precondition",
    )(spot, own, other, left, right)


def place_kernel(owners, slots, spot, targets, *rest):
    inputs, cluster = rest[:-1], rest[-1]
    quads = owners // 2
    here, side = spot[0], spot[1]
    block = owners * slots
    depth = cluster.shape[3]
    for source in range(owners):
        early, late = inputs[2 * source : 2 * source + 2]
        values = jnp.concatenate([early[...], late[...]], axis=0)
        count = values.shape[0]
        k, m = source % quads, source // quads
        producer = 2 * lax.bitwise_xor(here, k) + lax.bitwise_xor(side, m)
        slot_of = lax.broadcasted_iota(jnp.int32, (block, count), 0)
        placing = (slot_of == targets[source]).astype(jnp.bfloat16)
        placed = jnp.dot(placing, values, preferred_element_type=jnp.float32).astype(jnp.bfloat16)
        cluster[:, producer] = placed.reshape(owners, slots, depth)


def place(spot, targets, early, late, offset, slots):
    owners = len(early)
    first = early[0].shape[0]
    rest, features = late[0].shape
    depth = PLACE_WIDTH
    in_specs, operands = [pl.BlockSpec(targets.shape, lambda i, s: (0, 0, 0))], [targets]
    for a, b in zip(early, late):
        in_specs += [
            pl.BlockSpec((first, depth), lambda i, s: (0, offset // depth + i)),
            pl.BlockSpec((rest, depth), lambda i, s: (0, i)),
        ]
        operands += [a, b]
    return pl.pallas_call(
        functools.partial(place_kernel, owners, slots),
        grid_spec=pltpu.PrefetchScalarGridSpec(
            num_scalar_prefetch=1,
            grid=(features // depth,),
            in_specs=in_specs,
            out_specs=pl.BlockSpec((owners, owners, slots, depth), lambda i, s: (0, 0, 0, i)),
        ),
        out_shape=jax.ShapeDtypeStruct((owners, owners, slots, features), jnp.bfloat16),
        compiler_params=pltpu.CompilerParams(vmem_limit_bytes=VMEM_BYTES),
        cost_estimate=pl.CostEstimate(
            flops=2 * features * owners * slots * owners * (first + rest),
            bytes_accessed=owners * features * 2 * (first + rest + owners * slots),
            transcendentals=0,
        ),
        name="place",
    )(spot, *operands)


def tiles_kernel(count, spot, *rest):
    inputs, (keep, send) = rest[: 2 * count], rest[2 * count :]
    core = spot[2]
    owners, slots = inputs[0].shape[1:3]
    half = owners // 2
    rows = half * slots
    total = None
    for f in range(count):
        mine, ahead = inputs[2 * f], inputs[2 * f + 1]
        depth = mine.shape[3]
        halves = [
            ahead[0, pl.ds(lax.bitwise_xor(core, h) * half, half)].reshape(rows, depth)
            for h in range(2)
        ]
        product = lax.dot_general(
            jnp.concatenate(halves, axis=0),
            mine[0].reshape(owners * slots, depth),
            (((1,), (1,)), ((), ())),
            preferred_element_type=jnp.float32,
        )
        total = product if total is None else total + product
    keep[0] = total[:rows]
    send[0] = total[rows:]


def partial_tiles(spot, slices, order, j):
    owners, _, slots, _ = slices[0].shape
    block = owners * slots
    features = sum(s.shape[3] for s in slices)

    def owner_at(i, s):
        k = functools.reduce(lambda v, n: jnp.where(i == n, order[n], v), range(len(order)), 0)
        return 2 * lax.bitwise_xor(s[0], k) + s[1]

    def mine(i, s):
        return (owner_at(i, s), 0, 0, 0)

    def ahead(i, s):
        return (lax.rem(owner_at(i, s) + j + 1, owners), 0, 0, 0)

    in_specs, operands = [], []
    for part in slices:
        shape = (1,) + part.shape[1:]
        in_specs += [pl.BlockSpec(shape, mine), pl.BlockSpec(shape, ahead)]
        operands += [part, part]
    out = (len(order), block // 2, block)
    return pl.pallas_call(
        functools.partial(tiles_kernel, len(slices)),
        grid_spec=pltpu.PrefetchScalarGridSpec(
            num_scalar_prefetch=1,
            grid=(len(order),),
            in_specs=in_specs,
            out_specs=[pl.BlockSpec((1,) + out[1:], lambda i, s: (i, 0, 0))] * 2,
        ),
        out_shape=[jax.ShapeDtypeStruct(out, jnp.float32)] * 2,
        compiler_params=pltpu.CompilerParams(vmem_limit_bytes=VMEM_BYTES),
        cost_estimate=pl.CostEstimate(
            flops=2 * features * block * block * len(order),
            bytes_accessed=len(order) * block * (features * 4 + block * 4),
            transcendentals=0,
        ),
        name="partial_tiles",
    )(spot, *operands)


def split_plan(gradients, owner_of, pair_flags, left_factor, right_factor):
    count, half, width = gradients.shape
    feat = 2 * half * width
    owners = lax.axis_size("blk")
    quads = owners // 2
    reach = pair_flags.shape[1]
    slots = 3 * count // (2 * owners)
    block = owners * slots
    index = lax.axis_index("blk")
    core = lax.axis_index("dim")
    here, side = index // 2, index % 2
    spot = jnp.stack([here, side, core]).astype(jnp.int32)

    def across(x):
        return lax.ppermute(x, "dim", [(0, 1), (1, 0)])

    def along(x, k):
        return lax.ppermute(x, "blk", [(i, i ^ (2 * k)) for i in range(owners)])

    def beside(x):
        return lax.ppermute(x, "blk", [(i, i ^ 1) for i in range(owners)])

    def send(parts):
        got = [parts[0]] + [None] * (quads - 1)
        for k in reversed(range(1, quads)):
            got[k] = along(parts[k], k)
        return got

    swapped = jnp.concatenate([left_factor[half:], left_factor[:half]], axis=0)
    swapped = jnp.concatenate([swapped[:, half:], swapped[:, :half]], axis=1)
    left = jnp.where(core == 0, left_factor, swapped)
    right = jnp.concatenate([right_factor] * 3, axis=0)

    first = FIRST
    own_features = half * width // quads
    widths = [own_features * n // sum(SLICES) for n in SLICES]
    other_first = across(gradients[:first])
    other = across(gradients)
    *parts, mean_early = precondition(
        spot, gradients, other_first, left, right, (0, first, first), [own_features], quads
    )
    early = send(parts)
    *parts, mean_late = precondition(
        spot, gradients, other, left, right, (first, count - first, STEP), widths, quads
    )
    early_came = early[:1] + after(early[1:], parts[0])
    arrived = [early_came]
    besides = [[beside(part) for part in early_came]]

    means = jnp.concatenate([mean_early[:, 0], mean_late[:, 0]])
    told = jnp.stack([owner_of[:, 0].astype(jnp.float32), jnp.log1p(means)])
    told = jnp.stack(send([told] * quads))
    told = jnp.stack([told, beside(told)], axis=1)
    owners_all, influences = told[:, :, 0].astype(jnp.int32), told[:, :, 1]
    same = owners_all[..., :, None] == owners_all[..., None, :]
    before = jnp.arange(count)[:, None] > jnp.arange(count)[None, :]
    rank = jnp.sum((same & before).astype(jnp.int32), axis=-1)
    targets = owners_all * slots + rank

    slices = []
    offset = 0
    for f, wide in enumerate(widths):
        message = parts[f :: len(widths)]
        if f >= 1:
            message = after(message, *besides[f - 1])
        if f >= 2:
            message = after(message, slices[f - 2])
        late = send(message)
        if f == len(widths) - 1:
            late = late[:1] + after(late[1:], slices[f - 1])
        besides.append([beside(part) for part in late])
        slices.append(
            place(
                spot,
                targets.swapaxes(0, 1).reshape(owners, 1, count),
                early_came + besides[0],
                late + besides[-1],
                offset,
                slots,
            )
        )
        offset += wide

    flags = lax.dynamic_index_in_dim(pair_flags, index, 0, keepdims=False).astype(jnp.float32)
    ahead, behind = [], []
    pair = [list(reversed(range(1, quads, 2))), list(reversed(range(0, quads, 2)))]
    operands = slices
    for j in range(reach):
        keep_odd, send_odd = partial_tiles(spot, operands, pair[0], j)
        odd = keep_odd + across(send_odd)
        keep_even, send_even = partial_tiles(spot, operands, pair[1], j)
        came = along(odd, 1)
        if j + 1 < reach:
            operands = after(slices, odd, send_even)
        total = keep_even + across(send_even) + came
        while total.shape[0] > 1:
            rows = total.shape[0] // 2
            total = total[rows:] + along(total[:rows], 2 * rows)
        tile = (total[0] * (flags[j] * feat ** (-0.5))).astype(jnp.bfloat16)
        ahead.append(tile)
        turned = tile.T.reshape(2, block // 2, block // 2)
        straight = lax.dynamic_index_in_dim(turned, core, 0, keepdims=False)
        crossed = lax.dynamic_index_in_dim(turned, 1 - core, 0, keepdims=False)
        by = j + 1
        straight = from_behind(straight, "blk", by)
        crossed = lax.ppermute(
            crossed,
            ("blk", "dim"),
            [(2 * i + c, 2 * ((i + by) % owners) + 1 - c) for i in range(owners) for c in range(2)],
        )
        behind.append(
            jnp.where(
                core == 0,
                jnp.concatenate([straight, crossed], axis=1),
                jnp.concatenate([crossed, straight], axis=1),
            )
        )
    tiles = jnp.stack(ahead + behind).swapaxes(1, 2)

    (influences,) = after([influences], ahead[-1])
    wanted = index * slots + jnp.arange(slots, dtype=jnp.int32)
    chosen = targets[:, :, None, :] == wanted[:, None]
    self_influence = jnp.sum(jnp.where(chosen, influences[:, :, None, :], 0.0), axis=3)
    self_influence = lax.switch(
        index,
        [
            functools.partial(
                lambda i, x: jnp.stack(
                    [x[(p ^ i) // 2, (p ^ i) % 2] for p in range(owners)]
                ).astype(jnp.bfloat16),
                i,
            )
            for i in range(owners)
        ],
        self_influence,
    )
    return (tiles, self_influence.reshape(block))


def solution(mesh):
    owners = mesh.shape["blk"]

    def per_device(gradients, owner_of, pair_flags, left_factor, right_factor):
        block = 3 * gradients.shape[0] // 2
        partial_bytes = 4 * owners * pair_flags.shape[1] * block * block // 2
        quads = owners // 2
        fits = partial_bytes <= PARTIAL_BYTES and quads & (quads - 1) == 0
        plan = split_plan if fits and gradients.shape[0] % FIRST == 0 else ring_plan
        return plan(gradients, owner_of, pair_flags, left_factor, right_factor)

    return jax.shard_map(
        per_device,
        mesh=mesh,
        in_specs=(
            P(("groups", "blk"), "dim", None),
            P(("groups", "blk"), None),
            P("groups", None),
            P(),
            P(),
        ),
        out_specs=(P(("groups", "blk"), None, "dim"), P(("groups", "blk"))),
        check_vma=False,
    )
```

```python
import functools

import jax
import jax.numpy as jnp
from jax import lax
from jax.experimental import pallas as pl
from jax.experimental.pallas import tpu as pltpu
from jax.sharding import PartitionSpec as P

PARTIAL_BYTES = 16 * 2**20
FIRST = 64
SLICES = (3, 3, 2)
NOTE = 16
NOTE_BASE = 256
GROUP = 8
STEP = 32
VMEM_BYTES = 56 * 2**20
SMALL_COST = pl.CostEstimate(flops=2**20, bytes_accessed=2**16, transcendentals=0)


def from_behind(shard, axis, by):
    peers = lax.axis_size(axis)
    return lax.ppermute(shard, axis, [(i, (i + by) % peers) for i in range(peers)])


def slot_targets(owner_of, owners_count, slots):
    owners = owner_of[:, 0]
    onehot = (owners[:, None] == jnp.arange(owners_count, dtype=jnp.int32)[None, :]).astype(
        jnp.int32
    )
    earlier = jnp.cumsum(onehot, axis=0) - onehot
    rank = jnp.sum(earlier * onehot, axis=1)
    return owners * slots + rank


def ring_plan(gradients, owner_of, pair_flags, left_factor, right_factor):
    count, half, width = gradients.shape
    halves = lax.axis_size("dim")
    position = lax.axis_index("dim")
    feat = half * width * halves
    highest = lax.Precision.HIGHEST
    whole = lax.all_gather(gradients, "dim", axis=1, tiled=True)
    left_rows = lax.dynamic_slice_in_dim(left_factor, position * half, half, 0)
    left_side = jnp.einsum("ik,ekc->eic", left_rows, whole, preferred_element_type=jnp.float32)
    full = jnp.einsum("eic,cd->eid", left_side, right_factor.astype(jnp.float32), precision=highest)
    mean_sq = lax.psum(jnp.sum(full * full, axis=(1, 2)), "dim") / feat
    normed = (
        (full * lax.rsqrt(mean_sq + 1e-06)[:, None, None])
        .astype(jnp.bfloat16)
        .reshape(count, half * width)
    )
    influence = jnp.log1p(mean_sq).astype(jnp.bfloat16)
    owners_count = lax.axis_size("blk")
    slots = 3 * count // (2 * owners_count)
    block = owners_count * slots
    target = slot_targets(owner_of, owners_count, slots)
    placing = (jnp.arange(block, dtype=jnp.int32)[:, None] == target[None, :]).astype(jnp.bfloat16)
    outgoing = jnp.dot(placing, normed, preferred_element_type=jnp.float32).astype(jnp.bfloat16)
    outgoing = outgoing.reshape(owners_count, slots, half * width)
    sent_influence = jnp.dot(placing, influence, preferred_element_type=jnp.float32).astype(
        jnp.bfloat16
    )
    sent_influence = sent_influence.reshape(owners_count, slots)
    received, got_influence = (
        lax.all_to_all(outgoing, "blk", split_axis=0, concat_axis=0, tiled=True),
        lax.all_to_all(sent_influence, "blk", split_axis=0, concat_axis=0, tiled=True),
    )
    own = received.reshape(block, half * width)
    self_influence = got_influence.reshape(block)
    reach = pair_flags.shape[1]
    owner_index = lax.axis_index("blk")
    picker = (jnp.arange(owners_count, dtype=jnp.int32) == owner_index).astype(jnp.float32)
    flags = pair_flags.astype(jnp.float32)
    ahead_flags = jnp.dot(picker, flags)
    scale = feat ** (-0.5)
    partials = []
    for step in range(1, reach + 1):
        ahead = from_behind(own, "blk", -step)
        product = jnp.dot(own, ahead.T, preferred_element_type=jnp.float32)
        partials.append(product * (ahead_flags[step - 1] * scale))
    partials = partials + [term.T for term in partials]
    summed = lax.psum_scatter(jnp.stack(partials), "dim", scatter_dimension=2, tiled=True).astype(
        jnp.bfloat16
    )
    returned = [from_behind(summed[reach + step - 1], "blk", step) for step in range(1, reach + 1)]
    summed = jnp.concatenate([summed[:reach], jnp.stack(returned)], axis=0)
    return (summed, self_influence)


def after(values, *deps):
    return list(lax.optimization_barrier((tuple(values), deps))[0])


def precondition_kernel(plan, notes, spot, own, other, left, right, *rest):
    full, sums, parts = rest[-3:]
    if notes:
        slot_note, means_before, *outs, means, mean_sq = rest[:-3]
    else:
        *outs, mean_sq = rest[:-3]
    here, core = spot[0], spot[2]
    batch, half, width = own.shape
    side = 2 * half
    quads = len(plan)
    straight = left[...]
    turned = jnp.concatenate([straight[half:], straight[:half]], axis=0)
    turned = jnp.concatenate([turned[:, half:], turned[:, :half]], axis=1)
    factor = jnp.where(core == 0, straight, turned)
    right_twice = jnp.concatenate([right[...]] * 2, axis=0)
    for first in range(0, batch, GROUP):
        for e in range(first, first + GROUP, 2):
            pair = [jnp.concatenate([own[i], other[i]], axis=0) for i in (e, e + 1)]
            sides = jnp.dot(
                factor, jnp.concatenate(pair, axis=1), preferred_element_type=jnp.float32
            )
            for i in range(2):
                term = sides[:, i * width : (i + 1) * width]
                high = term.astype(jnp.bfloat16)
                low = (term - high.astype(jnp.float32)).astype(jnp.bfloat16)
                parts[pl.ds((e - first + i) * side, side), :] = jnp.concatenate(
                    [high, low], axis=1
                )
        product = jnp.dot(parts[...], right_twice, preferred_element_type=jnp.float32)
        full[pl.ds(first * side, GROUP * side), :] = product
        squares = (product * product).reshape(GROUP, side // 8, 8, width)
        sums[pl.ds(first * 8, GROUP * 8), :] = jnp.sum(squares, axis=1).reshape(GROUP * 8, width)
    total = sums[pl.ds(0, batch, stride=8), :]
    for s in range(1, 8):
        total = total + sums[pl.ds(s, batch, stride=8), :]
    mean = jnp.sum(total, axis=1, keepdims=True) / (side * width)
    spread_mean = jnp.broadcast_to(mean, (batch, width))
    step, steps = pl.program_id(0), pl.num_programs(0)
    at = pl.ds(pl.multiple_of(step * batch, batch), batch)
    mean_sq[at] = spread_mean
    scale = lax.rsqrt(spread_mean + 1e-06)
    slices = iter(outs)
    for k in range(quads):
        base = lax.bitwise_xor(here, k) * (half // quads)
        row = 0
        for wide in plan[k]:
            out = next(slices)
            for r in range(wide // width):
                values = full[pl.ds(base + row, batch, stride=side), :]
                out[at, r * width : (r + 1) * width] = (values * scale).astype(jnp.bfloat16)
                row += 1
    if notes:

        @pl.when(step == steps - 1)
        def _():
            every = jnp.concatenate([means_before[...], mean_sq[...]], axis=0)
            means[...] = every
            eye = lax.broadcasted_iota(jnp.int32, (width, width), 0) == lax.broadcasted_iota(
                jnp.int32, (width, width), 1
            )
            lanes = [
                jnp.sum(jnp.where(eye, every[i : i + width], 0.0), axis=0, keepdims=True)
                for i in range(0, every.shape[0], width)
            ]
            term = jnp.concatenate(lanes, axis=1)
            terms = []
            for _ in range(3):
                terms.append(term.astype(jnp.bfloat16).astype(jnp.float32))
                term = term - terms[-1]
            number = lax.broadcasted_iota(jnp.int32, (NOTE, every.shape[0]), 0)
            note = slot_note[...].astype(jnp.float32)
            for i in range(3):
                note = jnp.where(number == 2 + i, terms[i], note)
            slices = iter(outs)
            for k in range(quads):
                out = next(slices)
                rows = out.shape[0] - NOTE
                out[rows:, :] = jnp.zeros((NOTE, out.shape[1]), jnp.bfloat16)
                out[rows:, : every.shape[0]] = note.astype(jnp.bfloat16)
                for _ in plan[k][1:]:
                    next(slices)


def precondition(spot, own, other, left, right, span, plan, slot_note=None, means_before=None):
    _, half, width = own.shape
    side = 2 * half
    first, count, batch = span
    notes = slot_note is not None
    gradient_spec = pl.BlockSpec((batch, half, width), lambda i, s: (first // batch + i, 0, 0))
    whole = lambda shape: pl.BlockSpec(shape, lambda i, s: (0, 0))
    in_specs = [gradient_spec, gradient_spec, whole((side, side)), whole((width, width))]
    operands = [own, other, left, right]
    if notes:
        in_specs += [whole(slot_note.shape), whole(means_before.shape)]
        operands += [slot_note, means_before]
    out_shape = [
        jax.ShapeDtypeStruct((count + (NOTE if notes and f == 0 else 0), wide), jnp.bfloat16)
        for widths in plan
        for f, wide in enumerate(widths)
    ]
    if notes:
        out_shape.append(jax.ShapeDtypeStruct((first + count, width), jnp.float32))
    out_shape.append(jax.ShapeDtypeStruct((count, width), jnp.float32))
    return pl.pallas_call(
        functools.partial(precondition_kernel, plan, notes),
        grid_spec=pltpu.PrefetchScalarGridSpec(
            num_scalar_prefetch=1,
            grid=(count // batch,),
            in_specs=in_specs,
            out_specs=[whole(out.shape) for out in out_shape],
            scratch_shapes=[
                pltpu.VMEM((batch * side, width), jnp.float32),
                pltpu.VMEM((batch * 8, width), jnp.float32),
                pltpu.VMEM((GROUP * side, 2 * width), jnp.bfloat16),
            ],
        ),
        out_shape=out_shape,
        compiler_params=pltpu.CompilerParams(vmem_limit_bytes=VMEM_BYTES),
        cost_estimate=SMALL_COST,
        name="precondition",
    )(spot, *operands)


def tiles_kernel(order, reach, shapes, based, spot, *rest):
    owners, slots, early_rows, late_rows = shapes
    quads = owners // 2
    block = owners * slots
    notes, inputs = rest[:owners], rest[owners : 3 * owners]
    bases = rest[3 * owners : 3 * owners + 2 * reach] if based else ()
    outs, cluster = rest[-2 * reach - 1 : -1], rest[-1]
    here, side, core = spot[0], spot[1], spot[2]
    count = early_rows + late_rows
    depth = cluster.shape[3]
    step = pl.program_id(0)

    @pl.when(step == 0)
    def _():
        for source in range(owners):
            note = notes[source][:, :count].astype(jnp.float32).astype(jnp.int32)
            target = note[0:1] + note[1:2] * NOTE_BASE
            slot_of = lax.broadcasted_iota(jnp.int32, (block, count), 0)
            placing = (slot_of == target).astype(jnp.bfloat16)
            early, late = inputs[2 * source : 2 * source + 2]
            values = jnp.concatenate([early[...], late[:late_rows]], axis=0)
            k, m = source % quads, source // quads
            producer = 2 * lax.bitwise_xor(here, k) + lax.bitwise_xor(side, m)
            placed = jnp.dot(placing, values, preferred_element_type=jnp.float32)
            cluster[:, producer] = placed.astype(jnp.bfloat16).reshape(owners, slots, depth)

    half = owners // 2
    rows = half * slots

    @pl.when(step > 0)
    def _():
        k = functools.reduce(lambda v, n: jnp.where(step == n + 1, order[n], v), range(quads), 0)
        owner = 2 * lax.bitwise_xor(here, k) + side
        ahead = [
            cluster[
                lax.rem(owner + j + 1, owners), pl.ds(lax.bitwise_xor(core, h) * half, half)
            ].reshape(rows, depth)
            for h in range(2)
            for j in range(reach)
        ]
        product = lax.dot_general(
            jnp.concatenate(ahead, axis=0),
            cluster[owner].reshape(block, depth),
            (((1,), (1,)), ((), ())),
            preferred_element_type=jnp.float32,
        )
        for i in range(2 * reach):
            part = product[i * rows : (i + 1) * rows]
            outs[i][0] = part + bases[i][0] if based else part


def partial_tiles(spot, notes, pieces, width, order, reach, slots, bases=()):
    owners = len(pieces)
    block = owners * slots
    early_rows, late_rows = pieces[0][0][1][1], pieces[0][1][1][1]
    in_specs, operands = [], []
    for array, row in notes:
        in_specs.append(
            pl.BlockSpec((NOTE, 2 * NOTE_BASE), functools.partial(lambda r, i, s: (r, 0), row // NOTE))
        )
        operands.append(array)
    for piece in pieces:
        for array, (row, rows), column in piece:
            if column % width or row % rows:
                array, column, row = array[row : row + rows, column : column + width], 0, 0
            in_specs.append(
                pl.BlockSpec(
                    (rows, width),
                    functools.partial(lambda r, c, i, s: (r, c), row // rows, column // width),
                )
            )
            operands.append(array)
    shape = (len(order), block // 2, block)
    tile_specs = [
        pl.BlockSpec((1,) + shape[1:], lambda i, s: (jnp.maximum(i - 1, 0), 0, 0))
    ] * (2 * reach)
    return pl.pallas_call(
        functools.partial(
            tiles_kernel, order, reach, (owners, slots, early_rows, late_rows), bool(bases)
        ),
        grid_spec=pltpu.PrefetchScalarGridSpec(
            num_scalar_prefetch=1,
            grid=(1 + len(order),),
            in_specs=in_specs + (tile_specs if bases else []),
            out_specs=tile_specs,
            scratch_shapes=[pltpu.VMEM((owners, owners, slots, width), jnp.bfloat16)],
        ),
        out_shape=[jax.ShapeDtypeStruct(shape, jnp.float32)] * (2 * reach),
        compiler_params=pltpu.CompilerParams(vmem_limit_bytes=VMEM_BYTES),
        cost_estimate=SMALL_COST,
        name="partial_tiles",
    )(spot, *operands, *bases)


def split_plan(gradients, owner_of, pair_flags, left_factor, right_factor):
    count, half, width = gradients.shape
    feat = 2 * half * width
    owners = lax.axis_size("blk")
    quads = owners // 2
    reach = pair_flags.shape[1]
    slots = 3 * count // (2 * owners)
    block = owners * slots
    index = lax.axis_index("blk")
    core = lax.axis_index("dim")
    here, side = index // 2, index % 2
    spot = jnp.stack([here, side, core]).astype(jnp.int32)

    def across(x):
        return lax.ppermute(x, "dim", [(0, 1), (1, 0)])

    def along(x, k):
        return lax.ppermute(x, "blk", [(i, i ^ (2 * k)) for i in range(owners)])

    def beside(x):
        return lax.ppermute(x, "blk", [(i, i ^ 1) for i in range(owners)])

    def send(parts):
        return [parts[0]] + [along(parts[k], k) for k in range(1, quads)]

    first = FIRST
    rest_count = count - first
    features = half * width // quads
    widths = [features * n // sum(SLICES) for n in SLICES]
    other_first = across(gradients[:first])
    (whole,) = after([gradients], other_first)
    other = across(whole)

    *parts, mean_early = precondition(
        spot,
        gradients,
        other_first,
        left_factor,
        right_factor,
        (0, first, first),
        [[features]] * quads,
    )
    target = slot_targets(owner_of, owners, slots)
    slot_note = jnp.stack([target % NOTE_BASE, target // NOTE_BASE] + [target] * (NOTE - 2))
    slot_note = slot_note.astype(jnp.bfloat16)

    *parts, mean_early, other, slot_note = after([*parts, mean_early, other, slot_note])
    early = send(parts)
    early.append(beside(early[0]))
    own, *parts, means, _ = precondition(
        spot,
        gradients,
        other,
        left_factor,
        right_factor,
        (first, rest_count, STEP),
        [[features]] + [widths] * (quads - 1),
        slot_note,
        mean_early,
    )
    *early, own = after([*early, own])
    parts = after(parts, own)
    early.append(beside(jnp.concatenate(early[1:quads], axis=0)))
    order = [3, 1, 2, 0] if quads == 4 else list(reversed(range(quads)))
    sums, notes, came, crossed = (), [], [], None
    offset = 0
    late = [None] * owners
    for f in range(len(widths) + 1):
        wide = widths[f] if f < len(widths) else 0
        next_came, ready, next_crossed = [], [], None
        if f < len(widths):
            next_came = [along(parts[(k - 1) * len(widths) + f], k) for k in range(1, quads)]
        if f == 0:
            next_crossed = beside(own)
        elif f < len(widths):
            next_crossed = beside(jnp.concatenate(came, axis=0))
        else:
            next_crossed = [beside(part) for part in came]
        if f >= 2:
            sums = partial_tiles(spot, notes, pieces, widths[f - 2], order, reach, slots, sums)
        tied = jax.tree.leaves((next_came, next_crossed, early, own, parts, sums))
        held = after(tied)
        structure = jax.tree.structure((next_came, next_crossed, early, own, parts, sums))
        next_came, next_crossed, early, own, parts, sums = jax.tree.unflatten(structure, held)
        if f == 0:
            own_beside = next_crossed
        else:
            rows = came[0].shape[0]
            if f < len(widths):
                far = [(next_crossed, rows * k) for k in range(quads - 1)]
            else:
                far = [(part, 0) for part in next_crossed]
            start = sum(widths[: f - 1])
            late = [(own, 0)] + [(part, 0) for part in came] + [(own_beside, 0)] + far
            first_rows = [(part, 0) for part in early[: quads + 1]]
            first_rows += [(early[quads + 1], first * k) for k in range(quads - 1)]
            if f == 1:
                notes = [(array, row + rest_count) for array, row in late]
            pieces = [
                (
                    (first_rows[s][0], (first_rows[s][1], first), start),
                    (late[s][0], (late[s][1], rest_count), 0 if s % quads else start),
                )
                for s in range(owners)
            ]
        came = next_came
    sums = partial_tiles(spot, notes, pieces, widths[-1], order, reach, slots, sums)

    flags = lax.dynamic_index_in_dim(pair_flags, index, 0, keepdims=False).astype(jnp.float32)
    ahead, behind = [], []
    gathered = [across(sums[reach + j]) for j in range(reach)]
    for j in range(reach):
        total = {}
        keep, got = sums[j], gathered[j]
        if j < reach:
            odd = keep[: quads // 2] + got[: quads // 2]
            odd = along(odd, 1)
            for n, k in enumerate(order[quads // 2 :]):
                total[k] = keep[quads // 2 + n] + got[quads // 2 + n] + odd[n]
            total = total[0] + along(total[2], 2)
        else:
            for n, k in enumerate(order):
                total[k] = keep[n] + got[n]
            total = sum([along(total[k], k) for k in order[:-1]], total[0])
        tile = (total * (flags[j] * feat ** (-0.5))).astype(jnp.bfloat16)
        ahead.append(tile)
        turned = tile.T.reshape(2, block // 2, block // 2)
        straight = lax.dynamic_index_in_dim(turned, core, 0, keepdims=False)
        crossed = lax.dynamic_index_in_dim(turned, 1 - core, 0, keepdims=False)
        by = j + 1
        straight = from_behind(straight, "blk", by)
        crossed = lax.ppermute(
            crossed,
            ("blk", "dim"),
            [(2 * i + c, 2 * ((i + by) % owners) + 1 - c) for i in range(owners) for c in range(2)],
        )
        behind.append(
            jnp.where(
                core == 0,
                jnp.concatenate([straight, crossed], axis=1),
                jnp.concatenate([crossed, straight], axis=1),
            )
        )
    tiles = jnp.stack(ahead + behind).swapaxes(1, 2)

    note = jnp.stack([array[row : row + 5, :count] for array, row in notes]).astype(jnp.float32)
    targets = note[:, 0:1].astype(jnp.int32) + note[:, 1:2].astype(jnp.int32) * NOTE_BASE
    influences = jnp.log1p(note[:, 2:3] + note[:, 3:4] + note[:, 4:5])
    wanted = index * slots + jnp.arange(slots, dtype=jnp.int32)
    chosen = targets == wanted[None, :, None]
    self_influence = jnp.sum(jnp.where(chosen, influences, 0.0), axis=2)
    self_influence = lax.switch(
        index,
        [
            functools.partial(
                lambda i, x: jnp.stack(
                    [x[(p ^ i) // 2 + (p ^ i) % 2 * quads] for p in range(owners)]
                ).astype(jnp.bfloat16),
                i,
            )
            for i in range(owners)
        ],
        self_influence,
    )
    return (tiles, self_influence.reshape(block))


def solution(mesh):
    owners = mesh.shape["blk"]

    def per_device(gradients, owner_of, pair_flags, left_factor, right_factor):
        block = 3 * gradients.shape[0] // 2
        partial_bytes = 4 * owners * pair_flags.shape[1] * block * block // 2
        quads = owners // 2
        fits = partial_bytes <= PARTIAL_BYTES and quads == 4
        plan = split_plan if fits and gradients.shape[0] % FIRST == 0 else ring_plan
        return plan(gradients, owner_of, pair_flags, left_factor, right_factor)

    return jax.shard_map(
        per_device,
        mesh=mesh,
        in_specs=(
            P(("groups", "blk"), "dim", None),
            P(("groups", "blk"), None),
            P("groups", None),
            P(),
            P(),
        ),
        out_specs=(P(("groups", "blk"), None, "dim"), P(("groups", "blk"))),
        check_vma=False,
    )
```

```python
import functools

import jax
import jax.numpy as jnp
from jax import lax
from jax.experimental import pallas as pl
from jax.experimental.pallas import tpu as pltpu
from jax.sharding import PartitionSpec as P

PARTIAL_BYTES = 16 * 2**20
FIRST = 64
SLICES = (3, 3, 2)
NOTE = 16
NOTE_BASE = 256
GROUP = 8
STEP = 32
VMEM_BYTES = 30 * 2**20
SMALL_COST = pl.CostEstimate(flops=2**20, bytes_accessed=2**16, transcendentals=0)


def from_behind(shard, axis, by):
    peers = lax.axis_size(axis)
    return lax.ppermute(shard, axis, [(i, (i + by) % peers) for i in range(peers)])


def slot_targets(owner_of, owners_count, slots):
    owners = owner_of[:, 0]
    onehot = (owners[:, None] == jnp.arange(owners_count, dtype=jnp.int32)[None, :]).astype(
        jnp.int32
    )
    earlier = jnp.cumsum(onehot, axis=0) - onehot
    rank = jnp.sum(earlier * onehot, axis=1)
    return owners * slots + rank


def ring_plan(gradients, owner_of, pair_flags, left_factor, right_factor):
    count, half, width = gradients.shape
    halves = lax.axis_size("dim")
    position = lax.axis_index("dim")
    feat = half * width * halves
    highest = lax.Precision.HIGHEST
    whole = lax.all_gather(gradients, "dim", axis=1, tiled=True)
    left_rows = lax.dynamic_slice_in_dim(left_factor, position * half, half, 0)
    left_side = jnp.einsum("ik,ekc->eic", left_rows, whole, preferred_element_type=jnp.float32)
    full = jnp.einsum("eic,cd->eid", left_side, right_factor.astype(jnp.float32), precision=highest)
    mean_sq = lax.psum(jnp.sum(full * full, axis=(1, 2)), "dim") / feat
    normed = (
        (full * lax.rsqrt(mean_sq + 1e-06)[:, None, None])
        .astype(jnp.bfloat16)
        .reshape(count, half * width)
    )
    influence = jnp.log1p(mean_sq).astype(jnp.bfloat16)
    owners_count = lax.axis_size("blk")
    slots = 3 * count // (2 * owners_count)
    block = owners_count * slots
    target = slot_targets(owner_of, owners_count, slots)
    placing = (jnp.arange(block, dtype=jnp.int32)[:, None] == target[None, :]).astype(jnp.bfloat16)
    outgoing = jnp.dot(placing, normed, preferred_element_type=jnp.float32).astype(jnp.bfloat16)
    outgoing = outgoing.reshape(owners_count, slots, half * width)
    sent_influence = jnp.dot(placing, influence, preferred_element_type=jnp.float32).astype(
        jnp.bfloat16
    )
    sent_influence = sent_influence.reshape(owners_count, slots)
    received, got_influence = (
        lax.all_to_all(outgoing, "blk", split_axis=0, concat_axis=0, tiled=True),
        lax.all_to_all(sent_influence, "blk", split_axis=0, concat_axis=0, tiled=True),
    )
    own = received.reshape(block, half * width)
    self_influence = got_influence.reshape(block)
    reach = pair_flags.shape[1]
    owner_index = lax.axis_index("blk")
    picker = (jnp.arange(owners_count, dtype=jnp.int32) == owner_index).astype(jnp.float32)
    flags = pair_flags.astype(jnp.float32)
    ahead_flags = jnp.dot(picker, flags)
    scale = feat ** (-0.5)
    partials = []
    for step in range(1, reach + 1):
        ahead = from_behind(own, "blk", -step)
        product = jnp.dot(own, ahead.T, preferred_element_type=jnp.float32)
        partials.append(product * (ahead_flags[step - 1] * scale))
    partials = partials + [term.T for term in partials]
    summed = lax.psum_scatter(jnp.stack(partials), "dim", scatter_dimension=2, tiled=True).astype(
        jnp.bfloat16
    )
    returned = [from_behind(summed[reach + step - 1], "blk", step) for step in range(1, reach + 1)]
    summed = jnp.concatenate([summed[:reach], jnp.stack(returned)], axis=0)
    return (summed, self_influence)


def after(values, *deps):
    return list(lax.optimization_barrier((tuple(values), deps))[0])


def precondition_kernel(plan, notes, spot, own, other, left, right, *rest):
    full, sums, parts = rest[-3:]
    if notes:
        slot_note, means_before, *outs, means, mean_sq = rest[:-3]
    else:
        *outs, mean_sq = rest[:-3]
    here, core = spot[0], spot[2]
    batch, half, width = own.shape
    side = 2 * half
    quads = len(plan)
    straight = left[...]
    turned = jnp.concatenate([straight[half:], straight[:half]], axis=0)
    turned = jnp.concatenate([turned[:, half:], turned[:, :half]], axis=1)
    factor = jnp.where(core == 0, straight, turned)
    right_twice = jnp.concatenate([right[...]] * 2, axis=0)
    for first in range(0, batch, GROUP):
        for e in range(first, first + GROUP, 2):
            pair = [jnp.concatenate([own[i], other[i]], axis=0) for i in (e, e + 1)]
            sides = jnp.dot(
                factor, jnp.concatenate(pair, axis=1), preferred_element_type=jnp.float32
            )
            for i in range(2):
                term = sides[:, i * width : (i + 1) * width]
                high = term.astype(jnp.bfloat16)
                low = (term - high.astype(jnp.float32)).astype(jnp.bfloat16)
                parts[pl.ds((e - first + i) * side, side), :] = jnp.concatenate(
                    [high, low], axis=1
                )
        product = jnp.dot(parts[...], right_twice, preferred_element_type=jnp.float32)
        full[pl.ds(first * side, GROUP * side), :] = product
        squares = (product * product).reshape(GROUP, side // 8, 8, width)
        sums[pl.ds(first * 8, GROUP * 8), :] = jnp.sum(squares, axis=1).reshape(GROUP * 8, width)
    total = sums[pl.ds(0, batch, stride=8), :]
    for s in range(1, 8):
        total = total + sums[pl.ds(s, batch, stride=8), :]
    mean = jnp.sum(total, axis=1, keepdims=True) / (side * width)
    spread_mean = jnp.broadcast_to(mean, (batch, width))
    step, steps = pl.program_id(0), pl.num_programs(0)
    at = pl.ds(pl.multiple_of(step * batch, batch), batch)
    mean_sq[at] = spread_mean
    scale = lax.rsqrt(spread_mean + 1e-06)
    slices = iter(outs)
    for k in range(quads):
        base = lax.bitwise_xor(here, k) * (half // quads)
        row = 0
        for wide in plan[k]:
            out = next(slices)
            for r in range(wide // width):
                values = full[pl.ds(base + row, batch, stride=side), :]
                out[at, r * width : (r + 1) * width] = (values * scale).astype(jnp.bfloat16)
                row += 1
    if notes:

        @pl.when(step == steps - 1)
        def _():
            every = jnp.concatenate([means_before[...], mean_sq[...]], axis=0)
            means[...] = every
            eye = lax.broadcasted_iota(jnp.int32, (width, width), 0) == lax.broadcasted_iota(
                jnp.int32, (width, width), 1
            )
            lanes = [
                jnp.sum(jnp.where(eye, every[i : i + width], 0.0), axis=0, keepdims=True)
                for i in range(0, every.shape[0], width)
            ]
            term = jnp.concatenate(lanes, axis=1)
            terms = []
            for _ in range(3):
                terms.append(term.astype(jnp.bfloat16).astype(jnp.float32))
                term = term - terms[-1]
            number = lax.broadcasted_iota(jnp.int32, (NOTE, every.shape[0]), 0)
            note = slot_note[...].astype(jnp.float32)
            for i in range(3):
                note = jnp.where(number == 2 + i, terms[i], note)
            slices = iter(outs)
            for k in range(quads):
                out = next(slices)
                rows = out.shape[0] - NOTE
                out[rows:, :] = jnp.zeros((NOTE, out.shape[1]), jnp.bfloat16)
                out[rows:, : every.shape[0]] = note.astype(jnp.bfloat16)
                for _ in plan[k][1:]:
                    next(slices)


def precondition(spot, own, other, left, right, span, plan, slot_note=None, means_before=None):
    _, half, width = own.shape
    side = 2 * half
    first, count, batch = span
    notes = slot_note is not None
    gradient_spec = pl.BlockSpec((batch, half, width), lambda i, s: (first // batch + i, 0, 0))
    whole = lambda shape: pl.BlockSpec(shape, lambda i, s: (0, 0))
    in_specs = [gradient_spec, gradient_spec, whole((side, side)), whole((width, width))]
    operands = [own, other, left, right]
    if notes:
        in_specs += [whole(slot_note.shape), whole(means_before.shape)]
        operands += [slot_note, means_before]
    out_shape = [
        jax.ShapeDtypeStruct((count + (NOTE if notes and f == 0 else 0), wide), jnp.bfloat16)
        for widths in plan
        for f, wide in enumerate(widths)
    ]
    if notes:
        out_shape.append(jax.ShapeDtypeStruct((first + count, width), jnp.float32))
    out_shape.append(jax.ShapeDtypeStruct((count, width), jnp.float32))
    return pl.pallas_call(
        functools.partial(precondition_kernel, plan, notes),
        grid_spec=pltpu.PrefetchScalarGridSpec(
            num_scalar_prefetch=1,
            grid=(count // batch,),
            in_specs=in_specs,
            out_specs=[whole(out.shape) for out in out_shape],
            scratch_shapes=[
                pltpu.VMEM((batch * side, width), jnp.float32),
                pltpu.VMEM((batch * 8, width), jnp.float32),
                pltpu.VMEM((GROUP * side, 2 * width), jnp.bfloat16),
            ],
        ),
        out_shape=out_shape,
        compiler_params=pltpu.CompilerParams(vmem_limit_bytes=VMEM_BYTES),
        cost_estimate=SMALL_COST,
        name="precondition",
    )(spot, *operands)


def tiles_kernel(order, reach, shapes, based, spot, *rest):
    owners, slots, early_rows, late_rows = shapes
    quads = owners // 2
    block = owners * slots
    notes, inputs = rest[:owners], rest[owners : 3 * owners]
    bases = rest[3 * owners : 3 * owners + 2 * reach] if based else ()
    outs, cluster = rest[-2 * reach - 1 : -1], rest[-1]
    here, side, core = spot[0], spot[1], spot[2]
    count = early_rows + late_rows
    depth = cluster.shape[3]
    step = pl.program_id(0)

    @pl.when(step == 0)
    def _():
        for source in range(owners):
            note = notes[source][:, :count].astype(jnp.float32).astype(jnp.int32)
            target = note[0:1] + note[1:2] * NOTE_BASE
            slot_of = lax.broadcasted_iota(jnp.int32, (block, count), 0)
            placing = (slot_of == target).astype(jnp.bfloat16)
            early, late = inputs[2 * source : 2 * source + 2]
            values = jnp.concatenate([early[...], late[:late_rows]], axis=0)
            k, m = source % quads, source // quads
            producer = 2 * lax.bitwise_xor(here, k) + lax.bitwise_xor(side, m)
            placed = jnp.dot(placing, values, preferred_element_type=jnp.float32)
            cluster[:, producer] = placed.astype(jnp.bfloat16).reshape(owners, slots, depth)

    half = owners // 2
    rows = half * slots

    @pl.when(step > 0)
    def _():
        k = functools.reduce(lambda v, n: jnp.where(step == n + 1, order[n], v), range(quads), 0)
        owner = 2 * lax.bitwise_xor(here, k) + side
        ahead = [
            cluster[
                lax.rem(owner + j + 1, owners), pl.ds(lax.bitwise_xor(core, h) * half, half)
            ].reshape(rows, depth)
            for h in range(2)
            for j in range(reach)
        ]
        product = lax.dot_general(
            jnp.concatenate(ahead, axis=0),
            cluster[owner].reshape(block, depth),
            (((1,), (1,)), ((), ())),
            preferred_element_type=jnp.float32,
        )
        for i in range(2 * reach):
            part = product[i * rows : (i + 1) * rows]
            outs[i][0] = part + bases[i][0] if based else part


def partial_tiles(spot, notes, pieces, width, order, reach, slots, bases=()):
    owners = len(pieces)
    block = owners * slots
    early_rows, late_rows = pieces[0][0][1][1], pieces[0][1][1][1]
    in_specs, operands = [], []
    for array, row in notes:
        in_specs.append(
            pl.BlockSpec((NOTE, 2 * NOTE_BASE), functools.partial(lambda r, i, s: (r, 0), row // NOTE))
        )
        operands.append(array)
    for piece in pieces:
        for array, (row, rows), column in piece:
            if column % width or row % rows:
                array, column, row = array[row : row + rows, column : column + width], 0, 0
            in_specs.append(
                pl.BlockSpec(
                    (rows, width),
                    functools.partial(lambda r, c, i, s: (r, c), row // rows, column // width),
                )
            )
            operands.append(array)
    shape = (len(order), block // 2, block)
    tile_specs = [
        pl.BlockSpec((1,) + shape[1:], lambda i, s: (jnp.maximum(i - 1, 0), 0, 0))
    ] * (2 * reach)
    return pl.pallas_call(
        functools.partial(
            tiles_kernel, order, reach, (owners, slots, early_rows, late_rows), bool(bases)
        ),
        grid_spec=pltpu.PrefetchScalarGridSpec(
            num_scalar_prefetch=1,
            grid=(1 + len(order),),
            in_specs=in_specs + (tile_specs if bases else []),
            out_specs=tile_specs,
            scratch_shapes=[pltpu.VMEM((owners, owners, slots, width), jnp.bfloat16)],
        ),
        out_shape=[jax.ShapeDtypeStruct(shape, jnp.float32)] * (2 * reach),
        compiler_params=pltpu.CompilerParams(vmem_limit_bytes=VMEM_BYTES),
        cost_estimate=SMALL_COST,
        name="partial_tiles",
    )(spot, *operands, *bases)


def finish_kernel(spot, flags, *rest):
    *terms, tile, straight, crossed = rest
    total = sum([term[...] for term in terms[1:]], terms[0][...])
    done = (total * flags[0]).astype(tile.dtype)
    tile[...] = done
    turned = done.astype(jnp.float32).T.astype(tile.dtype)
    half = turned.shape[0] // 2
    core = spot[2]
    first, second = turned[:half], turned[half:]
    straight[...] = jnp.where(core == 0, first, second)
    crossed[...] = jnp.where(core == 0, second, first)


def finish(spot, factor, terms):
    rows, block = terms[0].shape
    spec = lambda shape: pl.BlockSpec(shape, lambda i, s, f: (0, 0))
    out = [(rows, block), (rows, rows), (rows, rows)]
    return pl.pallas_call(
        finish_kernel,
        grid_spec=pltpu.PrefetchScalarGridSpec(
            num_scalar_prefetch=2,
            grid=(1,),
            in_specs=[spec(term.shape) for term in terms],
            out_specs=[spec(shape) for shape in out],
        ),
        out_shape=[jax.ShapeDtypeStruct(shape, jnp.bfloat16) for shape in out],
        compiler_params=pltpu.CompilerParams(vmem_limit_bytes=VMEM_BYTES),
        cost_estimate=SMALL_COST,
        name="finish",
    )(spot, factor, *terms)


def split_plan(gradients, owner_of, pair_flags, left_factor, right_factor):
    count, half, width = gradients.shape
    feat = 2 * half * width
    owners = lax.axis_size("blk")
    quads = owners // 2
    reach = pair_flags.shape[1]
    slots = 3 * count // (2 * owners)
    block = owners * slots
    index = lax.axis_index("blk")
    core = lax.axis_index("dim")
    here, side = index // 2, index % 2
    spot = jnp.stack([here, side, core]).astype(jnp.int32)

    def across(x):
        return lax.ppermute(x, "dim", [(0, 1), (1, 0)])

    def along(x, k):
        return lax.ppermute(x, "blk", [(i, i ^ (2 * k)) for i in range(owners)])

    def beside(x):
        return lax.ppermute(x, "blk", [(i, i ^ 1) for i in range(owners)])

    def send(parts):
        return [parts[0]] + [along(parts[k], k) for k in range(1, quads)]

    first = FIRST
    rest_count = count - first
    features = half * width // quads
    widths = [features * n // sum(SLICES) for n in SLICES]
    own_first = gradients[:first]
    other_first = across(own_first)
    (whole,) = after([gradients], other_first)
    other = across(whole)

    *parts, mean_early = precondition(
        spot,
        own_first,
        other_first,
        left_factor,
        right_factor,
        (0, first, first),
        [[features]] * quads,
    )
    target = slot_targets(owner_of, owners, slots)
    slot_note = jnp.stack([target % NOTE_BASE, target // NOTE_BASE] + [target] * (NOTE - 2))
    slot_note = slot_note.astype(jnp.bfloat16)

    *parts, mean_early, slot_note = after([*parts, mean_early, slot_note])
    early = send(parts)
    early.append(beside(early[0]))
    own, *parts, means, _ = precondition(
        spot,
        gradients,
        other,
        left_factor,
        right_factor,
        (first, rest_count, STEP),
        [[features]] + [widths] * (quads - 1),
        slot_note,
        mean_early,
    )
    *early, own = after([*early, own])
    parts = after(parts, own)
    order = [3, 1, 2, 0]
    sums, notes, came = (), [], []
    own_beside = None
    start = 0
    for f in range(len(widths) + 1):
        next_came = []
        if f < len(widths):
            next_came = [along(parts[(k - 1) * len(widths) + f], k) for k in range(1, quads)]
        if f == 0:
            own_beside = beside(own)
            early.append(beside(jnp.concatenate(early[1 : quads - 1], axis=0)))
        if f == 1:
            early.append(beside(early[quads - 1]))
        if f < len(widths):
            crossed = [beside(jnp.concatenate(came, axis=0))] if came else []
        else:
            crossed = [beside(part) for part in came]
        if f >= 2:
            sums = partial_tiles(spot, notes, pieces, widths[f - 2], order, reach, slots, sums)
        every = (next_came, came, crossed, early, own, own_beside, parts, list(sums))
        leaves, structure = jax.tree.flatten(every)
        every = jax.tree.unflatten(structure, after(leaves))
        next_came, came, crossed, early, own, own_beside, parts, sums = every
        if f:
            rows = came[0].shape[0]
            late = [(own, 0)] + [(part, 0) for part in came] + [(own_beside, 0)]
            late += [(crossed[0], rows * k) for k in range(quads - 1)][: len(came) * (f < len(widths))]
            late += [(part, 0) for part in crossed][: len(came) * (f == len(widths))]
            head = [(part, 0) for part in early[: quads + 1]]
            head += [(early[quads + 1], first * k) for k in range(quads - 2)] + [(early[-1], 0)]
            if f == 1:
                notes = [(array, row + rest_count) for array, row in late]
            start = sum(widths[: f - 1])
            pieces = [
                (
                    (head[s][0], (head[s][1], first), start),
                    (late[s][0], (late[s][1], rest_count), 0 if s % quads else start),
                )
                for s in range(owners)
            ]
        came = next_came
    sums = partial_tiles(spot, notes, pieces, widths[-1], order, reach, slots, sums)

    flags = lax.dynamic_index_in_dim(pair_flags, index, 0, keepdims=False).astype(jnp.float32)
    ahead, behind = [None] * reach, [None] * reach
    gathered = [across(sums[reach + j]) for j in reversed(range(reach))][::-1]
    def back(x, by, turn):
        pairs = [
            (2 * i + c, 2 * ((i + by) % owners) + (1 - c if turn else c))
            for i in range(owners)
            for c in range(2)
        ]
        return lax.ppermute(x, ("blk", "dim"), pairs)

    spans = list(reversed(range(reach)))
    odds, evens, nears, fars = {}, {}, {}, {}
    for j in spans:
        keep, got = sums[j], gathered[j]
        odds[j] = along(keep[: quads // 2] + got[: quads // 2], 1)
        evens[j] = [keep[2] + got[2], keep[3] + got[3]]

    def halve(j):
        nears[j] = evens[j][1] + odds[j][1]
        fars[j] = along(evens[j][0] + odds[j][0], 2)

    def complete(j):
        factor = (flags[j] * feat ** (-0.5)).reshape(1)
        ahead[j], straight, crossed = finish(spot, factor, [nears[j], fars[j]])
        straight, crossed = back(straight, j + 1, False), back(crossed, j + 1, True)
        behind[j] = [straight, crossed]

    for n, j in enumerate(spans):
        if n > 1:
            complete(spans[n - 2])
            (odds[j],) = after([odds[j]], ahead[spans[n - 2]], *behind[spans[n - 2]])
        halve(j)
    for n in range(max(0, reach - 2), reach):
        j = spans[n]
        complete(j)
    for j in range(reach):
        straight, crossed = behind[j]
        behind[j] = jnp.where(
            core == 0,
            jnp.concatenate([straight, crossed], axis=1),
            jnp.concatenate([crossed, straight], axis=1),
        )
    tiles = jnp.stack(ahead + behind).swapaxes(1, 2)

    held = after([array for array, _ in notes], ahead[-1])
    notes = [(array, row) for array, (_, row) in zip(held, notes)]
    note = jnp.stack([array[row : row + 5, :count] for array, row in notes]).astype(jnp.float32)
    targets = note[:, 0:1].astype(jnp.int32) + note[:, 1:2].astype(jnp.int32) * NOTE_BASE
    influences = jnp.log1p(note[:, 2:3] + note[:, 3:4] + note[:, 4:5])
    wanted = index * slots + jnp.arange(slots, dtype=jnp.int32)
    chosen = targets == wanted[None, :, None]
    self_influence = jnp.sum(jnp.where(chosen, influences, 0.0), axis=2)
    self_influence = lax.switch(
        index,
        [
            functools.partial(
                lambda i, x: jnp.stack(
                    [x[(p ^ i) // 2 + (p ^ i) % 2 * quads] for p in range(owners)]
                ).astype(jnp.bfloat16),
                i,
            )
            for i in range(owners)
        ],
        self_influence,
    )
    return (tiles, self_influence.reshape(block))


def solution(mesh):
    owners = mesh.shape["blk"]

    def per_device(gradients, owner_of, pair_flags, left_factor, right_factor):
        block = 3 * gradients.shape[0] // 2
        partial_bytes = 4 * owners * pair_flags.shape[1] * block * block // 2
        quads = owners // 2
        fits = partial_bytes <= PARTIAL_BYTES and quads == 4
        plan = split_plan if fits and (gradients.shape[0] - FIRST) % STEP == 0 and FIRST % STEP == 0 else ring_plan
        return plan(gradients, owner_of, pair_flags, left_factor, right_factor)

    return jax.shard_map(
        per_device,
        mesh=mesh,
        in_specs=(
            P(("groups", "blk"), "dim", None),
            P(("groups", "blk"), None),
            P("groups", None),
            P(),
            P(),
        ),
        out_specs=(P(("groups", "blk"), None, "dim"), P(("groups", "blk"))),
        check_vma=False,
    )
```

```python
import functools

import jax
import jax.numpy as jnp
from jax import lax
from jax.experimental import pallas as pl
from jax.experimental.pallas import tpu as pltpu
from jax.sharding import PartitionSpec as P

PARTIAL_BYTES = 16 * 2**20
FIRST = 64
SLICES = (3, 3, 2)
NOTE = 16
NOTE_BASE = 256
PARTS = ((2,), (0,), (1,))
GROUP = 8
STEP = 32
VMEM_BYTES = 30 * 2**20
SMALL_COST = pl.CostEstimate(flops=2**20, bytes_accessed=2**16, transcendentals=0)


def from_behind(shard, axis, by):
    peers = lax.axis_size(axis)
    return lax.ppermute(shard, axis, [(i, (i + by) % peers) for i in range(peers)])


def slot_targets(owner_of, owners_count, slots):
    owners = owner_of[:, 0]
    onehot = (owners[:, None] == jnp.arange(owners_count, dtype=jnp.int32)[None, :]).astype(
        jnp.int32
    )
    earlier = jnp.cumsum(onehot, axis=0) - onehot
    rank = jnp.sum(earlier * onehot, axis=1)
    return owners * slots + rank


def ring_plan(gradients, owner_of, pair_flags, left_factor, right_factor):
    count, half, width = gradients.shape
    halves = lax.axis_size("dim")
    position = lax.axis_index("dim")
    feat = half * width * halves
    highest = lax.Precision.HIGHEST
    whole = lax.all_gather(gradients, "dim", axis=1, tiled=True)
    left_rows = lax.dynamic_slice_in_dim(left_factor, position * half, half, 0)
    left_side = jnp.einsum("ik,ekc->eic", left_rows, whole, preferred_element_type=jnp.float32)
    full = jnp.einsum("eic,cd->eid", left_side, right_factor.astype(jnp.float32), precision=highest)
    mean_sq = lax.psum(jnp.sum(full * full, axis=(1, 2)), "dim") / feat
    normed = (
        (full * lax.rsqrt(mean_sq + 1e-06)[:, None, None])
        .astype(jnp.bfloat16)
        .reshape(count, half * width)
    )
    influence = jnp.log1p(mean_sq).astype(jnp.bfloat16)
    owners_count = lax.axis_size("blk")
    slots = 3 * count // (2 * owners_count)
    block = owners_count * slots
    target = slot_targets(owner_of, owners_count, slots)
    placing = (jnp.arange(block, dtype=jnp.int32)[:, None] == target[None, :]).astype(jnp.bfloat16)
    outgoing = jnp.dot(placing, normed, preferred_element_type=jnp.float32).astype(jnp.bfloat16)
    outgoing = outgoing.reshape(owners_count, slots, half * width)
    sent_influence = jnp.dot(placing, influence, preferred_element_type=jnp.float32).astype(
        jnp.bfloat16
    )
    sent_influence = sent_influence.reshape(owners_count, slots)
    received, got_influence = (
        lax.all_to_all(outgoing, "blk", split_axis=0, concat_axis=0, tiled=True),
        lax.all_to_all(sent_influence, "blk", split_axis=0, concat_axis=0, tiled=True),
    )
    own = received.reshape(block, half * width)
    self_influence = got_influence.reshape(block)
    reach = pair_flags.shape[1]
    owner_index = lax.axis_index("blk")
    picker = (jnp.arange(owners_count, dtype=jnp.int32) == owner_index).astype(jnp.float32)
    flags = pair_flags.astype(jnp.float32)
    ahead_flags = jnp.dot(picker, flags)
    scale = feat ** (-0.5)
    partials = []
    for step in range(1, reach + 1):
        ahead = from_behind(own, "blk", -step)
        product = jnp.dot(own, ahead.T, preferred_element_type=jnp.float32)
        partials.append(product * (ahead_flags[step - 1] * scale))
    partials = partials + [term.T for term in partials]
    summed = lax.psum_scatter(jnp.stack(partials), "dim", scatter_dimension=2, tiled=True).astype(
        jnp.bfloat16
    )
    returned = [from_behind(summed[reach + step - 1], "blk", step) for step in range(1, reach + 1)]
    summed = jnp.concatenate([summed[:reach], jnp.stack(returned)], axis=0)
    return (summed, self_influence)


def after(values, *deps):
    return list(lax.optimization_barrier((tuple(values), deps))[0])


def precondition_kernel(plan, notes, spot, own, other, left, right, *rest):
    full, sums, parts = rest[-3:]
    if notes:
        slot_note, means_before, *outs, means, mean_sq = rest[:-3]
    else:
        *outs, mean_sq = rest[:-3]
    here, core = spot[0], spot[2]
    batch, half, width = own.shape
    side = 2 * half
    quads = len(plan)
    straight = left[...]
    turned = jnp.concatenate([straight[half:], straight[:half]], axis=0)
    turned = jnp.concatenate([turned[:, half:], turned[:, :half]], axis=1)
    factor = jnp.where(core == 0, straight, turned)
    right_twice = jnp.concatenate([right[...]] * 2, axis=0)
    for first in range(0, batch, GROUP):
        for e in range(first, first + GROUP, 2):
            pair = [jnp.concatenate([own[i], other[i]], axis=0) for i in (e, e + 1)]
            sides = jnp.dot(
                factor, jnp.concatenate(pair, axis=1), preferred_element_type=jnp.float32
            )
            for i in range(2):
                term = sides[:, i * width : (i + 1) * width]
                high = term.astype(jnp.bfloat16)
                low = (term - high.astype(jnp.float32)).astype(jnp.bfloat16)
                parts[pl.ds((e - first + i) * side, side), :] = jnp.concatenate(
                    [high, low], axis=1
                )
        product = jnp.dot(parts[...], right_twice, preferred_element_type=jnp.float32)
        full[pl.ds(first * side, GROUP * side), :] = product
        squares = (product * product).reshape(GROUP, side // 8, 8, width)
        sums[pl.ds(first * 8, GROUP * 8), :] = jnp.sum(squares, axis=1).reshape(GROUP * 8, width)
    total = sums[pl.ds(0, batch, stride=8), :]
    for s in range(1, 8):
        total = total + sums[pl.ds(s, batch, stride=8), :]
    mean = jnp.sum(total, axis=1, keepdims=True) / (side * width)
    spread_mean = jnp.broadcast_to(mean, (batch, width))
    step, steps = pl.program_id(0), pl.num_programs(0)
    at = pl.ds(pl.multiple_of(step * batch, batch), batch)
    mean_sq[at] = spread_mean
    scale = lax.rsqrt(spread_mean + 1e-06)
    slices = iter(outs)
    for k in range(quads):
        base = lax.bitwise_xor(here, k) * (half // quads)
        row = 0
        for wide in plan[k]:
            out = next(slices)
            for r in range(wide // width):
                values = full[pl.ds(base + row, batch, stride=side), :]
                out[at, r * width : (r + 1) * width] = (values * scale).astype(jnp.bfloat16)
                row += 1
    if notes:

        @pl.when(step == steps - 1)
        def _():
            every = jnp.concatenate([means_before[...], mean_sq[...]], axis=0)
            means[...] = every
            eye = lax.broadcasted_iota(jnp.int32, (width, width), 0) == lax.broadcasted_iota(
                jnp.int32, (width, width), 1
            )
            lanes = [
                jnp.sum(jnp.where(eye, every[i : i + width], 0.0), axis=0, keepdims=True)
                for i in range(0, every.shape[0], width)
            ]
            term = jnp.concatenate(lanes, axis=1)
            terms = []
            for _ in range(3):
                terms.append(term.astype(jnp.bfloat16).astype(jnp.float32))
                term = term - terms[-1]
            number = lax.broadcasted_iota(jnp.int32, (NOTE, every.shape[0]), 0)
            note = slot_note[...].astype(jnp.float32)
            for i in range(3):
                note = jnp.where(number == 2 + i, terms[i], note)
            slices = iter(outs)
            for k in range(quads):
                out = next(slices)
                rows = out.shape[0] - NOTE
                out[rows:, :] = jnp.zeros((NOTE, out.shape[1]), jnp.bfloat16)
                out[rows:, : every.shape[0]] = note.astype(jnp.bfloat16)
                for _ in plan[k][1:]:
                    next(slices)


def precondition(spot, own, other, left, right, span, plan, slot_note=None, means_before=None):
    _, half, width = own.shape
    side = 2 * half
    first, count, batch = span
    notes = slot_note is not None
    gradient_spec = pl.BlockSpec((batch, half, width), lambda i, s: (first // batch + i, 0, 0))
    whole = lambda shape: pl.BlockSpec(shape, lambda i, s: (0, 0))
    in_specs = [gradient_spec, gradient_spec, whole((side, side)), whole((width, width))]
    operands = [own, other, left, right]
    if notes:
        in_specs += [whole(slot_note.shape), whole(means_before.shape)]
        operands += [slot_note, means_before]
    out_shape = [
        jax.ShapeDtypeStruct((count + (NOTE if notes and f == 0 else 0), wide), jnp.bfloat16)
        for widths in plan
        for f, wide in enumerate(widths)
    ]
    if notes:
        out_shape.append(jax.ShapeDtypeStruct((first + count, width), jnp.float32))
    out_shape.append(jax.ShapeDtypeStruct((count, width), jnp.float32))
    return pl.pallas_call(
        functools.partial(precondition_kernel, plan, notes),
        grid_spec=pltpu.PrefetchScalarGridSpec(
            num_scalar_prefetch=1,
            grid=(count // batch,),
            in_specs=in_specs,
            out_specs=[whole(out.shape) for out in out_shape],
            scratch_shapes=[
                pltpu.VMEM((batch * side, width), jnp.float32),
                pltpu.VMEM((batch * 8, width), jnp.float32),
                pltpu.VMEM((GROUP * side, 2 * width), jnp.bfloat16),
            ],
        ),
        out_shape=out_shape,
        compiler_params=pltpu.CompilerParams(vmem_limit_bytes=VMEM_BYTES),
        cost_estimate=SMALL_COST,
        name="precondition",
    )(spot, *operands)


def tiles_kernel(order, reach, shapes, based, spot, *rest):
    owners, slots, early_rows, late_rows = shapes
    quads = owners // 2
    block = owners * slots
    notes, inputs = rest[:owners], rest[owners : 3 * owners]
    bases = rest[3 * owners : 3 * owners + 2 * len(PARTS)] if based else ()
    outs, cluster = rest[-2 * len(PARTS) - 1 : -1], rest[-1]
    here, side, core = spot[0], spot[1], spot[2]
    count = early_rows + late_rows
    depth = cluster.shape[3]
    step = pl.program_id(0)

    @pl.when(step == 0)
    def _():
        for source in range(owners):
            note = notes[source][:, :count].astype(jnp.float32).astype(jnp.int32)
            target = note[0:1] + note[1:2] * NOTE_BASE
            slot_of = lax.broadcasted_iota(jnp.int32, (block, count), 0)
            placing = (slot_of == target).astype(jnp.bfloat16)
            early, late = inputs[2 * source : 2 * source + 2]
            values = jnp.concatenate([early[...], late[:late_rows]], axis=0)
            k, m = source % quads, source // quads
            producer = 2 * lax.bitwise_xor(here, k) + lax.bitwise_xor(side, m)
            placed = jnp.dot(placing, values, preferred_element_type=jnp.float32)
            cluster[:, producer] = placed.astype(jnp.bfloat16).reshape(owners, slots, depth)

    half = owners // 2
    rows = half * slots

    @pl.when(step > 0)
    def _():
        k = functools.reduce(lambda v, n: jnp.where(step == n + 1, order[n], v), range(quads), 0)
        owner = 2 * lax.bitwise_xor(here, k) + side
        ahead = [
            cluster[
                lax.rem(owner + j + 1, owners), pl.ds(lax.bitwise_xor(core, h) * half, half)
            ].reshape(rows, depth)
            for h in range(2)
            for j in range(reach)
        ]
        product = lax.dot_general(
            jnp.concatenate(ahead, axis=0),
            cluster[owner].reshape(block, depth),
            (((1,), (1,)), ((), ())),
            preferred_element_type=jnp.float32,
        )
        for h in range(2):
            for n, part in enumerate(PARTS):
                out = h * len(PARTS) + n
                for at, j in enumerate(part):
                    first = (h * reach + j) * rows
                    value = product[first : first + rows]
                    outs[out][0, at] = value + bases[out][0, at] if based else value


def partial_tiles(spot, notes, pieces, width, order, reach, slots, bases=()):
    owners = len(pieces)
    block = owners * slots
    early_rows, late_rows = pieces[0][0][1][1], pieces[0][1][1][1]
    in_specs, operands = [], []
    for array, row in notes:
        in_specs.append(
            pl.BlockSpec((NOTE, 2 * NOTE_BASE), functools.partial(lambda r, i, s: (r, 0), row // NOTE))
        )
        operands.append(array)
    for piece in pieces:
        for array, (row, rows), column in piece:
            if column % width or row % rows:
                array, column, row = array[row : row + rows, column : column + width], 0, 0
            in_specs.append(
                pl.BlockSpec(
                    (rows, width),
                    functools.partial(lambda r, c, i, s: (r, c), row // rows, column // width),
                )
            )
            operands.append(array)
    shapes = [(len(order), len(part), block // 2, block) for part in PARTS] * 2
    tile_specs = [
        pl.BlockSpec((1,) + shape[1:], lambda i, s: (jnp.maximum(i - 1, 0), 0, 0, 0))
        for shape in shapes
    ]
    return pl.pallas_call(
        functools.partial(
            tiles_kernel, order, reach, (owners, slots, early_rows, late_rows), bool(bases)
        ),
        grid_spec=pltpu.PrefetchScalarGridSpec(
            num_scalar_prefetch=1,
            grid=(1 + len(order),),
            in_specs=in_specs + (tile_specs if bases else []),
            out_specs=tile_specs,
            scratch_shapes=[pltpu.VMEM((owners, owners, slots, width), jnp.bfloat16)],
        ),
        out_shape=[jax.ShapeDtypeStruct(shape, jnp.float32) for shape in shapes],
        compiler_params=pltpu.CompilerParams(vmem_limit_bytes=VMEM_BYTES),
        cost_estimate=SMALL_COST,
        name="partial_tiles",
    )(spot, *operands, *bases)


def finish_kernel(spot, flags, *rest):
    *terms, tile, straight, crossed = rest
    total = terms[0][0] + terms[1][0]
    done = (total * flags[0]).astype(tile.dtype)
    tile[...] = done
    turned = done.astype(jnp.float32).T.astype(tile.dtype)
    half = turned.shape[0] // 2
    core = spot[2]
    first, second = turned[:half], turned[half:]
    straight[...] = jnp.where(core == 0, first, second)
    crossed[...] = jnp.where(core == 0, second, first)


def finish(spot, factor, terms, at):
    _, rows, block = terms[0].shape
    spec = lambda shape: pl.BlockSpec(shape, lambda i, s, f: (0, 0))
    out = [(rows, block), (rows, rows), (rows, rows)]
    return pl.pallas_call(
        finish_kernel,
        grid_spec=pltpu.PrefetchScalarGridSpec(
            num_scalar_prefetch=2,
            grid=(1,),
            in_specs=[pl.BlockSpec((1, rows, block), lambda i, s, f: (at, 0, 0))] * 2,
            out_specs=[spec(shape) for shape in out],
        ),
        out_shape=[jax.ShapeDtypeStruct(shape, jnp.bfloat16) for shape in out],
        compiler_params=pltpu.CompilerParams(vmem_limit_bytes=VMEM_BYTES),
        cost_estimate=SMALL_COST,
        name="finish",
    )(spot, factor, *terms)


def split_plan(gradients, owner_of, pair_flags, left_factor, right_factor):
    count, half, width = gradients.shape
    feat = 2 * half * width
    owners = lax.axis_size("blk")
    quads = owners // 2
    reach = pair_flags.shape[1]
    slots = 3 * count // (2 * owners)
    block = owners * slots
    index = lax.axis_index("blk")
    core = lax.axis_index("dim")
    here, side = index // 2, index % 2
    spot = jnp.stack([here, side, core]).astype(jnp.int32)

    def across(x):
        return lax.ppermute(x, "dim", [(0, 1), (1, 0)])

    def along(x, k):
        return lax.ppermute(x, "blk", [(i, i ^ (2 * k)) for i in range(owners)])

    def beside(x):
        return lax.ppermute(x, "blk", [(i, i ^ 1) for i in range(owners)])

    def send(parts):
        return [parts[0]] + [along(parts[k], k) for k in range(1, quads)]

    first = FIRST
    rest_count = count - first
    features = half * width // quads
    widths = [features * n // sum(SLICES) for n in SLICES]
    own_first = gradients[:first]
    other_first = across(own_first)
    (whole,) = after([gradients], other_first)
    other = across(whole)

    *parts, mean_early = precondition(
        spot,
        own_first,
        other_first,
        left_factor,
        right_factor,
        (0, first, first),
        [[features]] * quads,
    )
    target = slot_targets(owner_of, owners, slots)
    slot_note = jnp.stack([target % NOTE_BASE, target // NOTE_BASE] + [target] * (NOTE - 2))
    slot_note = slot_note.astype(jnp.bfloat16)

    *parts, mean_early, slot_note = after([*parts, mean_early, slot_note])
    early = send(parts)
    early.append(beside(early[0]))
    own, *parts, means, _ = precondition(
        spot,
        gradients,
        other,
        left_factor,
        right_factor,
        (first, rest_count, STEP),
        [[features]] + [widths] * (quads - 1),
        slot_note,
        mean_early,
    )
    *early, own = after([*early, own])
    parts = after(parts, own)
    order = [3, 1, 2, 0]
    sums, notes, came = (), [], []
    own_beside = None
    start = 0
    for f in range(len(widths) + 1):
        next_came = []
        if f < len(widths):
            next_came = [along(parts[(k - 1) * len(widths) + f], k) for k in range(1, quads)]
        if f == 0:
            own_beside = beside(own)
            early.append(beside(jnp.concatenate(early[1 : quads - 1], axis=0)))
        if f == 1:
            early.append(beside(early[quads - 1]))
        if f < len(widths):
            crossed = [beside(jnp.concatenate(came, axis=0))] if came else []
        else:
            crossed = [beside(part) for part in came]
        if f >= 2:
            sums = partial_tiles(spot, notes, pieces, widths[f - 2], order, reach, slots, sums)
        every = (next_came, came, crossed, early, own, own_beside, parts, list(sums))
        leaves, structure = jax.tree.flatten(every)
        every = jax.tree.unflatten(structure, after(leaves))
        next_came, came, crossed, early, own, own_beside, parts, sums = every
        if f:
            rows = came[0].shape[0]
            late = [(own, 0)] + [(part, 0) for part in came] + [(own_beside, 0)]
            late += [(crossed[0], rows * k) for k in range(quads - 1)][: len(came) * (f < len(widths))]
            late += [(part, 0) for part in crossed][: len(came) * (f == len(widths))]
            head = [(part, 0) for part in early[: quads + 1]]
            head += [(early[quads + 1], first * k) for k in range(quads - 2)] + [(early[-1], 0)]
            if f == 1:
                notes = [(array, row + rest_count) for array, row in late]
            start = sum(widths[: f - 1])
            pieces = [
                (
                    (head[s][0], (head[s][1], first), start),
                    (late[s][0], (late[s][1], rest_count), 0 if s % quads else start),
                )
                for s in range(owners)
            ]
        came = next_came
    sums = partial_tiles(spot, notes, pieces, widths[-1], order, reach, slots, sums)

    flags = lax.dynamic_index_in_dim(pair_flags, index, 0, keepdims=False).astype(jnp.float32)
    ahead, behind = [None] * reach, [None] * reach
    def back(x, by, turn):
        pairs = [
            (2 * i + c, 2 * ((i + by) % owners) + (1 - c if turn else c))
            for i in range(owners)
            for c in range(2)
        ]
        return lax.ppermute(x, ("blk", "dim"), pairs)

    keeps, gives = sums[: len(PARTS)], sums[len(PARTS) :]
    gots = [across(give) for give in gives]
    odds = [keep[:2] + got[:2] for keep, got in zip(keeps, gots)]
    odds = [along(odd, 1) for odd in odds] + [odds[-1]]
    evens = [[keep[2] + got[2], keep[3] + got[3]] for keep, got in zip(keeps, gots)]
    (odds[0],) = after([odds[0]], odds.pop())
    nears, fars = {}, {}

    def halve(n):
        nears[n] = evens[n][1] + odds[n][1]
        fars[n] = along(evens[n][0] + odds[n][0], 2)

    def complete(n):
        for at, j in enumerate(PARTS[n]):
            factor = (flags[j] * feat ** (-0.5)).reshape(1)
            ahead[j], straight, crossed = finish(spot, factor, [nears[n], fars[n]], at)
            behind[j] = [back(straight, j + 1, False), back(crossed, j + 1, True)]

    last = len(PARTS) - 1
    for n in range(last):
        halve(n)
    complete(0)
    waits = [behind[j][0] for j in PARTS[0]]
    (odds[last],) = after([odds[last]], *waits)
    halve(last)
    for n in range(1, last + 1):
        complete(n)
    for j in range(reach):
        straight, crossed = behind[j]
        behind[j] = jnp.where(
            core == 0,
            jnp.concatenate([straight, crossed], axis=1),
            jnp.concatenate([crossed, straight], axis=1),
        )
    tiles = jnp.stack(ahead + behind).swapaxes(1, 2)

    held = after([array for array, _ in notes], ahead[-1])
    notes = [(array, row) for array, (_, row) in zip(held, notes)]
    note = jnp.stack([array[row : row + 5, :count] for array, row in notes]).astype(jnp.float32)
    targets = note[:, 0:1].astype(jnp.int32) + note[:, 1:2].astype(jnp.int32) * NOTE_BASE
    influences = jnp.log1p(note[:, 2:3] + note[:, 3:4] + note[:, 4:5])
    wanted = index * slots + jnp.arange(slots, dtype=jnp.int32)
    chosen = targets == wanted[None, :, None]
    self_influence = jnp.sum(jnp.where(chosen, influences, 0.0), axis=2)
    self_influence = lax.switch(
        index,
        [
            functools.partial(
                lambda i, x: jnp.stack(
                    [x[(p ^ i) // 2 + (p ^ i) % 2 * quads] for p in range(owners)]
                ).astype(jnp.bfloat16),
                i,
            )
            for i in range(owners)
        ],
        self_influence,
    )
    return (tiles, self_influence.reshape(block))


def solution(mesh):
    owners = mesh.shape["blk"]

    def per_device(gradients, owner_of, pair_flags, left_factor, right_factor):
        block = 3 * gradients.shape[0] // 2
        partial_bytes = 4 * owners * pair_flags.shape[1] * block * block // 2
        quads = owners // 2
        fits = partial_bytes <= PARTIAL_BYTES and quads == 4
        plan = split_plan if fits and (gradients.shape[0] - FIRST) % STEP == 0 and FIRST % STEP == 0 else ring_plan
        return plan(gradients, owner_of, pair_flags, left_factor, right_factor)

    return jax.shard_map(
        per_device,
        mesh=mesh,
        in_specs=(
            P(("groups", "blk"), "dim", None),
            P(("groups", "blk"), None),
            P("groups", None),
            P(),
            P(),
        ),
        out_specs=(P(("groups", "blk"), None, "dim"), P(("groups", "blk"))),
        check_vma=False,
    )
```

```python
import functools

import jax
import jax.numpy as jnp
from jax import lax
from jax.experimental import pallas as pl
from jax.experimental.pallas import tpu as pltpu
from jax.sharding import PartitionSpec as P

PARTIAL_BYTES = 16 * 2**20
FIRST = 64
SLICES = (3, 3, 2)
NOTE = 16
NOTE_BASE = 256
PARTS = ((2,), (0,), (1,))
GROUP = 8
STEP = 32
VMEM_BYTES = 30 * 2**20
SMALL_COST = pl.CostEstimate(flops=2**20, bytes_accessed=2**16, transcendentals=0)


def from_behind(shard, axis, by):
    peers = lax.axis_size(axis)
    return lax.ppermute(shard, axis, [(i, (i + by) % peers) for i in range(peers)])


def slot_targets(owner_of, owners_count, slots):
    owners = owner_of[:, 0]
    onehot = (owners[:, None] == jnp.arange(owners_count, dtype=jnp.int32)[None, :]).astype(
        jnp.int32
    )
    earlier = jnp.cumsum(onehot, axis=0) - onehot
    rank = jnp.sum(earlier * onehot, axis=1)
    return owners * slots + rank


def ring_plan(gradients, owner_of, pair_flags, left_factor, right_factor):
    count, half, width = gradients.shape
    halves = lax.axis_size("dim")
    position = lax.axis_index("dim")
    feat = half * width * halves
    highest = lax.Precision.HIGHEST
    whole = lax.all_gather(gradients, "dim", axis=1, tiled=True)
    left_rows = lax.dynamic_slice_in_dim(left_factor, position * half, half, 0)
    left_side = jnp.einsum("ik,ekc->eic", left_rows, whole, preferred_element_type=jnp.float32)
    full = jnp.einsum("eic,cd->eid", left_side, right_factor.astype(jnp.float32), precision=highest)
    mean_sq = lax.psum(jnp.sum(full * full, axis=(1, 2)), "dim") / feat
    normed = (
        (full * lax.rsqrt(mean_sq + 1e-06)[:, None, None])
        .astype(jnp.bfloat16)
        .reshape(count, half * width)
    )
    influence = jnp.log1p(mean_sq).astype(jnp.bfloat16)
    owners_count = lax.axis_size("blk")
    slots = 3 * count // (2 * owners_count)
    block = owners_count * slots
    target = slot_targets(owner_of, owners_count, slots)
    placing = (jnp.arange(block, dtype=jnp.int32)[:, None] == target[None, :]).astype(jnp.bfloat16)
    outgoing = jnp.dot(placing, normed, preferred_element_type=jnp.float32).astype(jnp.bfloat16)
    outgoing = outgoing.reshape(owners_count, slots, half * width)
    sent_influence = jnp.dot(placing, influence, preferred_element_type=jnp.float32).astype(
        jnp.bfloat16
    )
    sent_influence = sent_influence.reshape(owners_count, slots)
    received, got_influence = (
        lax.all_to_all(outgoing, "blk", split_axis=0, concat_axis=0, tiled=True),
        lax.all_to_all(sent_influence, "blk", split_axis=0, concat_axis=0, tiled=True),
    )
    own = received.reshape(block, half * width)
    self_influence = got_influence.reshape(block)
    reach = pair_flags.shape[1]
    owner_index = lax.axis_index("blk")
    picker = (jnp.arange(owners_count, dtype=jnp.int32) == owner_index).astype(jnp.float32)
    flags = pair_flags.astype(jnp.float32)
    ahead_flags = jnp.dot(picker, flags)
    scale = feat ** (-0.5)
    partials = []
    for step in range(1, reach + 1):
        ahead = from_behind(own, "blk", -step)
        product = jnp.dot(own, ahead.T, preferred_element_type=jnp.float32)
        partials.append(product * (ahead_flags[step - 1] * scale))
    partials = partials + [term.T for term in partials]
    summed = lax.psum_scatter(jnp.stack(partials), "dim", scatter_dimension=2, tiled=True).astype(
        jnp.bfloat16
    )
    returned = [from_behind(summed[reach + step - 1], "blk", step) for step in range(1, reach + 1)]
    summed = jnp.concatenate([summed[:reach], jnp.stack(returned)], axis=0)
    return (summed, self_influence)


def after(values, *deps):
    return list(lax.optimization_barrier((tuple(values), deps))[0])


def precondition_kernel(plan, notes, spot, own, other, left, right, *rest):
    full, sums, parts = rest[-3:]
    if notes:
        slot_note, means_before, *outs, means, mean_sq = rest[:-3]
    else:
        *outs, mean_sq = rest[:-3]
    here, core = spot[0], spot[2]
    batch, half, width = own.shape
    side = 2 * half
    quads = len(plan)
    straight = left[...]
    turned = jnp.concatenate([straight[half:], straight[:half]], axis=0)
    turned = jnp.concatenate([turned[:, half:], turned[:, :half]], axis=1)
    factor = jnp.where(core == 0, straight, turned)
    right_twice = jnp.concatenate([right[...]] * 2, axis=0)
    for first in range(0, batch, GROUP):
        for e in range(first, first + GROUP, 2):
            pair = [jnp.concatenate([own[i], other[i]], axis=0) for i in (e, e + 1)]
            sides = jnp.dot(
                factor, jnp.concatenate(pair, axis=1), preferred_element_type=jnp.float32
            )
            for i in range(2):
                term = sides[:, i * width : (i + 1) * width]
                high = term.astype(jnp.bfloat16)
                low = (term - high.astype(jnp.float32)).astype(jnp.bfloat16)
                parts[pl.ds((e - first + i) * side, side), :] = jnp.concatenate(
                    [high, low], axis=1
                )
        product = jnp.dot(parts[...], right_twice, preferred_element_type=jnp.float32)
        full[pl.ds(first * side, GROUP * side), :] = product
        squares = (product * product).reshape(GROUP, side // 8, 8, width)
        sums[pl.ds(first * 8, GROUP * 8), :] = jnp.sum(squares, axis=1).reshape(GROUP * 8, width)
    total = sums[pl.ds(0, batch, stride=8), :]
    for s in range(1, 8):
        total = total + sums[pl.ds(s, batch, stride=8), :]
    mean = jnp.sum(total, axis=1, keepdims=True) / (side * width)
    spread_mean = jnp.broadcast_to(mean, (batch, width))
    step, steps = pl.program_id(0), pl.num_programs(0)
    at = pl.ds(pl.multiple_of(step * batch, batch), batch)
    mean_sq[at] = spread_mean
    scale = lax.rsqrt(spread_mean + 1e-06)
    slices = iter(outs)
    for k in range(quads):
        base = lax.bitwise_xor(here, k) * (half // quads)
        row = 0
        for wide in plan[k]:
            out = next(slices)
            for r in range(wide // width):
                values = full[pl.ds(base + row, batch, stride=side), :]
                out[at, r * width : (r + 1) * width] = (values * scale).astype(jnp.bfloat16)
                row += 1
    if notes:

        @pl.when(step == steps - 1)
        def _():
            every = jnp.concatenate([means_before[...], mean_sq[...]], axis=0)
            means[...] = every
            eye = lax.broadcasted_iota(jnp.int32, (width, width), 0) == lax.broadcasted_iota(
                jnp.int32, (width, width), 1
            )
            lanes = [
                jnp.sum(jnp.where(eye, every[i : i + width], 0.0), axis=0, keepdims=True)
                for i in range(0, every.shape[0], width)
            ]
            term = jnp.concatenate(lanes, axis=1)
            terms = []
            for _ in range(3):
                terms.append(term.astype(jnp.bfloat16).astype(jnp.float32))
                term = term - terms[-1]
            number = lax.broadcasted_iota(jnp.int32, (NOTE, every.shape[0]), 0)
            note = slot_note[...].astype(jnp.float32)
            for i in range(3):
                note = jnp.where(number == 2 + i, terms[i], note)
            slices = iter(outs)
            for k in range(quads):
                out = next(slices)
                rows = out.shape[0] - NOTE
                out[rows:, :] = jnp.zeros((NOTE, out.shape[1]), jnp.bfloat16)
                out[rows:, : every.shape[0]] = note.astype(jnp.bfloat16)
                for _ in plan[k][1:]:
                    next(slices)


def precondition(spot, own, other, left, right, span, plan, slot_note=None, means_before=None):
    _, half, width = own.shape
    side = 2 * half
    first, count, batch = span
    notes = slot_note is not None
    gradient_spec = pl.BlockSpec((batch, half, width), lambda i, s: (first // batch + i, 0, 0))
    whole = lambda shape: pl.BlockSpec(shape, lambda i, s: (0, 0))
    in_specs = [gradient_spec, gradient_spec, whole((side, side)), whole((width, width))]
    operands = [own, other, left, right]
    if notes:
        in_specs += [whole(slot_note.shape), whole(means_before.shape)]
        operands += [slot_note, means_before]
    out_shape = [
        jax.ShapeDtypeStruct((count + (NOTE if notes and f == 0 else 0), wide), jnp.bfloat16)
        for widths in plan
        for f, wide in enumerate(widths)
    ]
    if notes:
        out_shape.append(jax.ShapeDtypeStruct((first + count, width), jnp.float32))
    out_shape.append(jax.ShapeDtypeStruct((count, width), jnp.float32))
    return pl.pallas_call(
        functools.partial(precondition_kernel, plan, notes),
        grid_spec=pltpu.PrefetchScalarGridSpec(
            num_scalar_prefetch=1,
            grid=(count // batch,),
            in_specs=in_specs,
            out_specs=[whole(out.shape) for out in out_shape],
            scratch_shapes=[
                pltpu.VMEM(((batch + 1) * side, width), jnp.float32),
                pltpu.VMEM(((batch + 1) * 8, width), jnp.float32),
                pltpu.VMEM((GROUP * side, 2 * width), jnp.bfloat16),
            ],
        ),
        out_shape=out_shape,
        compiler_params=pltpu.CompilerParams(vmem_limit_bytes=VMEM_BYTES),
        cost_estimate=SMALL_COST,
        name="precondition",
    )(spot, *operands)


def tiles_kernel(order, reach, shapes, based, spot, *rest):
    owners, slots, early_rows, late_rows = shapes
    quads = owners // 2
    block = owners * slots
    notes, inputs = rest[:owners], rest[owners : 3 * owners]
    bases = rest[3 * owners : 3 * owners + 2 * len(PARTS)] if based else ()
    outs, cluster = rest[-2 * len(PARTS) - 1 : -1], rest[-1]
    here, side, core = spot[0], spot[1], spot[2]
    count = early_rows + late_rows
    depth = cluster.shape[3]
    step = pl.program_id(0)

    @pl.when(step == 0)
    def _():
        for source in range(owners):
            note = notes[source][:, :count].astype(jnp.float32).astype(jnp.int32)
            target = note[0:1] + note[1:2] * NOTE_BASE
            slot_of = lax.broadcasted_iota(jnp.int32, (block, count), 0)
            placing = (slot_of == target).astype(jnp.bfloat16)
            early, late = inputs[2 * source : 2 * source + 2]
            values = jnp.concatenate([early[...], late[:late_rows]], axis=0)
            k, m = source % quads, source // quads
            producer = 2 * lax.bitwise_xor(here, k) + lax.bitwise_xor(side, m)
            placed = jnp.dot(placing, values, preferred_element_type=jnp.float32)
            cluster[:, producer] = placed.astype(jnp.bfloat16).reshape(owners, slots, depth)

    half = owners // 2
    rows = half * slots

    @pl.when(step > 0)
    def _():
        k = functools.reduce(lambda v, n: jnp.where(step == n + 1, order[n], v), range(quads), 0)
        owner = 2 * lax.bitwise_xor(here, k) + side
        ahead = [
            cluster[
                lax.rem(owner + j + 1, owners), pl.ds(lax.bitwise_xor(core, h) * half, half)
            ].reshape(rows, depth)
            for h in range(2)
            for j in range(reach)
        ]
        product = lax.dot_general(
            jnp.concatenate(ahead, axis=0),
            cluster[owner].reshape(block, depth),
            (((1,), (1,)), ((), ())),
            preferred_element_type=jnp.float32,
        )
        for h in range(2):
            for n, part in enumerate(PARTS):
                out = h * len(PARTS) + n
                for at, j in enumerate(part):
                    first = (h * reach + j) * rows
                    value = product[first : first + rows]
                    outs[out][0, at] = value + bases[out][0, at] if based else value


def partial_tiles(spot, notes, pieces, width, order, reach, slots, bases=()):
    owners = len(pieces)
    block = owners * slots
    early_rows, late_rows = pieces[0][0][1][1], pieces[0][1][1][1]
    in_specs, operands = [], []
    for array, row in notes:
        in_specs.append(
            pl.BlockSpec((NOTE, 2 * NOTE_BASE), functools.partial(lambda r, i, s: (r, 0), row // NOTE))
        )
        operands.append(array)
    for piece in pieces:
        for array, (row, rows), column in piece:
            if column % width or row % rows:
                array, column, row = array[row : row + rows, column : column + width], 0, 0
            in_specs.append(
                pl.BlockSpec(
                    (rows, width),
                    functools.partial(lambda r, c, i, s: (r, c), row // rows, column // width),
                )
            )
            operands.append(array)
    shapes = [(len(order), len(part), block // 2, block) for part in PARTS] * 2
    tile_specs = [
        pl.BlockSpec((1,) + shape[1:], lambda i, s: (jnp.maximum(i - 1, 0), 0, 0, 0))
        for shape in shapes
    ]
    return pl.pallas_call(
        functools.partial(
            tiles_kernel, order, reach, (owners, slots, early_rows, late_rows), bool(bases)
        ),
        grid_spec=pltpu.PrefetchScalarGridSpec(
            num_scalar_prefetch=1,
            grid=(1 + len(order),),
            in_specs=in_specs + (tile_specs if bases else []),
            out_specs=tile_specs,
            scratch_shapes=[pltpu.VMEM((owners, owners, slots, width), jnp.bfloat16)],
        ),
        out_shape=[jax.ShapeDtypeStruct(shape, jnp.float32) for shape in shapes],
        compiler_params=pltpu.CompilerParams(vmem_limit_bytes=VMEM_BYTES),
        cost_estimate=SMALL_COST,
        name="partial_tiles",
    )(spot, *operands, *bases)


def finish_kernel(spot, flags, *rest):
    *terms, tile, straight, crossed = rest
    total = terms[0][0] + terms[1][0]
    done = (total * flags[0]).astype(tile.dtype)
    tile[...] = done
    turned = done.astype(jnp.float32).T.astype(tile.dtype)
    half = turned.shape[0] // 2
    core = spot[2]
    first, second = turned[:half], turned[half:]
    straight[...] = jnp.where(core == 0, first, second)
    crossed[...] = jnp.where(core == 0, second, first)


def finish(spot, factor, terms, at):
    _, rows, block = terms[0].shape
    spec = lambda shape: pl.BlockSpec(shape, lambda i, s, f: (0, 0))
    out = [(rows, block), (rows, rows), (rows, rows)]
    return pl.pallas_call(
        finish_kernel,
        grid_spec=pltpu.PrefetchScalarGridSpec(
            num_scalar_prefetch=2,
            grid=(1,),
            in_specs=[pl.BlockSpec((1, rows, block), lambda i, s, f: (at, 0, 0))] * 2,
            out_specs=[spec(shape) for shape in out],
        ),
        out_shape=[jax.ShapeDtypeStruct(shape, jnp.bfloat16) for shape in out],
        compiler_params=pltpu.CompilerParams(vmem_limit_bytes=VMEM_BYTES),
        cost_estimate=SMALL_COST,
        name="finish",
    )(spot, factor, *terms)


def split_plan(gradients, owner_of, pair_flags, left_factor, right_factor):
    count, half, width = gradients.shape
    feat = 2 * half * width
    owners = lax.axis_size("blk")
    quads = owners // 2
    reach = pair_flags.shape[1]
    slots = 3 * count // (2 * owners)
    block = owners * slots
    index = lax.axis_index("blk")
    core = lax.axis_index("dim")
    here, side = index // 2, index % 2
    spot = jnp.stack([here, side, core]).astype(jnp.int32)

    def across(x):
        return lax.ppermute(x, "dim", [(0, 1), (1, 0)])

    def along(x, k):
        return lax.ppermute(x, "blk", [(i, i ^ (2 * k)) for i in range(owners)])

    def beside(x):
        return lax.ppermute(x, "blk", [(i, i ^ 1) for i in range(owners)])

    def send(parts):
        return [parts[0]] + [along(parts[k], k) for k in range(1, quads)]

    first = FIRST
    rest_count = count - first
    features = half * width // quads
    widths = [features * n // sum(SLICES) for n in SLICES]
    own_first = gradients[:first]
    other_first = across(own_first)
    (whole,) = after([gradients], other_first)
    other = across(whole)

    *parts, mean_early = precondition(
        spot,
        own_first,
        other_first,
        left_factor,
        right_factor,
        (0, first, first),
        [[features]] * quads,
    )
    target = slot_targets(owner_of, owners, slots)
    slot_note = jnp.stack([target % NOTE_BASE, target // NOTE_BASE] + [target] * (NOTE - 2))
    slot_note = slot_note.astype(jnp.bfloat16)

    *parts, mean_early, slot_note = after([*parts, mean_early, slot_note])
    early = send(parts)
    early.append(beside(early[0]))
    own, *parts, means, _ = precondition(
        spot,
        gradients,
        other,
        left_factor,
        right_factor,
        (first, rest_count, STEP),
        [[features]] + [widths] * (quads - 1),
        slot_note,
        mean_early,
    )
    *early, own = after([*early, own])
    parts = after(parts, own)
    order = [3, 1, 2, 0]
    sums, notes, came = (), [], []
    own_beside = None
    start = 0
    for f in range(len(widths) + 1):
        next_came = []
        if f < len(widths):
            next_came = [along(parts[(k - 1) * len(widths) + f], k) for k in range(1, quads)]
        if f == 0:
            own_beside = beside(own)
            early.append(beside(jnp.concatenate(early[1 : quads - 1], axis=0)))
        if f == 1:
            early.append(beside(early[quads - 1]))
        if f < len(widths):
            crossed = [beside(jnp.concatenate(came, axis=0))] if came else []
        else:
            crossed = [beside(part) for part in came]
        if f >= 2:
            sums = partial_tiles(spot, notes, pieces, widths[f - 2], order, reach, slots, sums)
        every = (next_came, came, crossed, early, own, own_beside, parts, list(sums))
        leaves, structure = jax.tree.flatten(every)
        every = jax.tree.unflatten(structure, after(leaves))
        next_came, came, crossed, early, own, own_beside, parts, sums = every
        if f:
            rows = came[0].shape[0]
            late = [(own, 0)] + [(part, 0) for part in came] + [(own_beside, 0)]
            late += [(crossed[0], rows * k) for k in range(quads - 1)][: len(came) * (f < len(widths))]
            late += [(part, 0) for part in crossed][: len(came) * (f == len(widths))]
            head = [(part, 0) for part in early[: quads + 1]]
            head += [(early[quads + 1], first * k) for k in range(quads - 2)] + [(early[-1], 0)]
            if f == 1:
                notes = [(array, row + rest_count) for array, row in late]
            start = sum(widths[: f - 1])
            pieces = [
                (
                    (head[s][0], (head[s][1], first), start),
                    (late[s][0], (late[s][1], rest_count), 0 if s % quads else start),
                )
                for s in range(owners)
            ]
        came = next_came
    sums = partial_tiles(spot, notes, pieces, widths[-1], order, reach, slots, sums)

    flags = lax.dynamic_index_in_dim(pair_flags, index, 0, keepdims=False).astype(jnp.float32)
    ahead, behind = [None] * reach, [None] * reach
    def back(x, by, turn):
        pairs = [
            (2 * i + c, 2 * ((i + by) % owners) + (1 - c if turn else c))
            for i in range(owners)
            for c in range(2)
        ]
        return lax.ppermute(x, ("blk", "dim"), pairs)

    keeps, gives = sums[: len(PARTS)], sums[len(PARTS) :]
    gots = [across(give) for give in gives]
    odds = [keep[:2] + got[:2] for keep, got in zip(keeps, gots)]
    odds = [along(odd, 1) for odd in odds] + [odds[-1]]
    evens = [[keep[2] + got[2], keep[3] + got[3]] for keep, got in zip(keeps, gots)]
    (odds[0],) = after([odds[0]], odds.pop())
    nears, fars = {}, {}

    def halve(n):
        nears[n] = evens[n][1] + odds[n][1]
        fars[n] = along(evens[n][0] + odds[n][0], 2)

    def complete(n):
        for at, j in enumerate(PARTS[n]):
            factor = (flags[j] * feat ** (-0.5)).reshape(1)
            ahead[j], straight, crossed = finish(spot, factor, [nears[n], fars[n]], at)
            behind[j] = [back(straight, j + 1, False), back(crossed, j + 1, True)]

    last = len(PARTS) - 1
    for n in range(last):
        halve(n)
    complete(0)
    waits = [behind[j][0] for j in PARTS[0]]
    (odds[last],) = after([odds[last]], *waits)
    halve(last)
    for n in range(1, last + 1):
        complete(n)
    for j in range(reach):
        straight, crossed = behind[j]
        behind[j] = jnp.where(
            core == 0,
            jnp.concatenate([straight, crossed], axis=1),
            jnp.concatenate([crossed, straight], axis=1),
        )
    tiles = jnp.stack(ahead + behind).swapaxes(1, 2)

    held = after([array for array, _ in notes], ahead[-1])
    notes = [(array, row) for array, (_, row) in zip(held, notes)]
    note = jnp.stack([array[row : row + 5, :count] for array, row in notes]).astype(jnp.float32)
    targets = note[:, 0:1].astype(jnp.int32) + note[:, 1:2].astype(jnp.int32) * NOTE_BASE
    influences = jnp.log1p(note[:, 2:3] + note[:, 3:4] + note[:, 4:5])
    wanted = index * slots + jnp.arange(slots, dtype=jnp.int32)
    chosen = targets == wanted[None, :, None]
    self_influence = jnp.sum(jnp.where(chosen, influences, 0.0), axis=2)
    self_influence = lax.switch(
        index,
        [
            functools.partial(
                lambda i, x: jnp.stack(
                    [x[(p ^ i) // 2 + (p ^ i) % 2 * quads] for p in range(owners)]
                ).astype(jnp.bfloat16),
                i,
            )
            for i in range(owners)
        ],
        self_influence,
    )
    return (tiles, self_influence.reshape(block))


def solution(mesh):
    owners = mesh.shape["blk"]

    def per_device(gradients, owner_of, pair_flags, left_factor, right_factor):
        block = 3 * gradients.shape[0] // 2
        partial_bytes = 4 * owners * pair_flags.shape[1] * block * block // 2
        quads = owners // 2
        fits = partial_bytes <= PARTIAL_BYTES and quads == 4
        plan = split_plan if fits and (gradients.shape[0] - FIRST) % STEP == 0 and FIRST % STEP == 0 else ring_plan
        return plan(gradients, owner_of, pair_flags, left_factor, right_factor)

    return jax.shard_map(
        per_device,
        mesh=mesh,
        in_specs=(
            P(("groups", "blk"), "dim", None),
            P(("groups", "blk"), None),
            P("groups", None),
            P(),
            P(),
        ),
        out_specs=(P(("groups", "blk"), None, "dim"), P(("groups", "blk"))),
        check_vma=False,
    )
```

```python
import functools

import jax
import jax.numpy as jnp
from jax import lax
from jax.experimental import pallas as pl
from jax.experimental.pallas import tpu as pltpu
from jax.sharding import PartitionSpec as P

PARTIAL_BYTES = 16 * 2**20
FIRST = 64
SLICES = (3, 3, 2)
NOTE = 16
NOTE_BASE = 256
PARTS = ((2,), (0,), (1,))
GROUP = 8
STEP = 32
VMEM_BYTES = 22 * 2**20
SMALL_COST = pl.CostEstimate(flops=2**20, bytes_accessed=2**16, transcendentals=0)


def from_behind(shard, axis, by):
    peers = lax.axis_size(axis)
    return lax.ppermute(shard, axis, [(i, (i + by) % peers) for i in range(peers)])


def slot_targets(owner_of, owners_count, slots):
    owners = owner_of[:, 0]
    onehot = (owners[:, None] == jnp.arange(owners_count, dtype=jnp.int32)[None, :]).astype(
        jnp.int32
    )
    earlier = jnp.cumsum(onehot, axis=0) - onehot
    rank = jnp.sum(earlier * onehot, axis=1)
    return owners * slots + rank


def ring_plan(gradients, owner_of, pair_flags, left_factor, right_factor):
    count, half, width = gradients.shape
    halves = lax.axis_size("dim")
    position = lax.axis_index("dim")
    feat = half * width * halves
    highest = lax.Precision.HIGHEST
    whole = lax.all_gather(gradients, "dim", axis=1, tiled=True)
    left_rows = lax.dynamic_slice_in_dim(left_factor, position * half, half, 0)
    left_side = jnp.einsum("ik,ekc->eic", left_rows, whole, preferred_element_type=jnp.float32)
    full = jnp.einsum("eic,cd->eid", left_side, right_factor.astype(jnp.float32), precision=highest)
    mean_sq = lax.psum(jnp.sum(full * full, axis=(1, 2)), "dim") / feat
    normed = (
        (full * lax.rsqrt(mean_sq + 1e-06)[:, None, None])
        .astype(jnp.bfloat16)
        .reshape(count, half * width)
    )
    influence = jnp.log1p(mean_sq).astype(jnp.bfloat16)
    owners_count = lax.axis_size("blk")
    slots = 3 * count // (2 * owners_count)
    block = owners_count * slots
    target = slot_targets(owner_of, owners_count, slots)
    placing = (jnp.arange(block, dtype=jnp.int32)[:, None] == target[None, :]).astype(jnp.bfloat16)
    outgoing = jnp.dot(placing, normed, preferred_element_type=jnp.float32).astype(jnp.bfloat16)
    outgoing = outgoing.reshape(owners_count, slots, half * width)
    sent_influence = jnp.dot(placing, influence, preferred_element_type=jnp.float32).astype(
        jnp.bfloat16
    )
    sent_influence = sent_influence.reshape(owners_count, slots)
    received, got_influence = (
        lax.all_to_all(outgoing, "blk", split_axis=0, concat_axis=0, tiled=True),
        lax.all_to_all(sent_influence, "blk", split_axis=0, concat_axis=0, tiled=True),
    )
    own = received.reshape(block, half * width)
    self_influence = got_influence.reshape(block)
    reach = pair_flags.shape[1]
    owner_index = lax.axis_index("blk")
    picker = (jnp.arange(owners_count, dtype=jnp.int32) == owner_index).astype(jnp.float32)
    flags = pair_flags.astype(jnp.float32)
    ahead_flags = jnp.dot(picker, flags)
    scale = feat ** (-0.5)
    partials = []
    for step in range(1, reach + 1):
        ahead = from_behind(own, "blk", -step)
        product = jnp.dot(own, ahead.T, preferred_element_type=jnp.float32)
        partials.append(product * (ahead_flags[step - 1] * scale))
    partials = partials + [term.T for term in partials]
    summed = lax.psum_scatter(jnp.stack(partials), "dim", scatter_dimension=2, tiled=True).astype(
        jnp.bfloat16
    )
    returned = [from_behind(summed[reach + step - 1], "blk", step) for step in range(1, reach + 1)]
    summed = jnp.concatenate([summed[:reach], jnp.stack(returned)], axis=0)
    return (summed, self_influence)


def after(values, *deps):
    return list(lax.optimization_barrier((tuple(values), deps))[0])


def precondition_kernel(plan, notes, spot, own, other, left, right, *rest):
    full, sums, parts = rest[-3:]
    if notes:
        slot_note, means_before, *outs, means, mean_sq = rest[:-3]
    else:
        *outs, mean_sq = rest[:-3]
    here, core = spot[0], spot[2]
    batch, half, width = own.shape
    side = 2 * half
    quads = len(plan)
    straight = left[...]
    turned = jnp.concatenate([straight[half:], straight[:half]], axis=0)
    turned = jnp.concatenate([turned[:, half:], turned[:, :half]], axis=1)
    factor = jnp.where(core == 0, straight, turned)
    right_twice = jnp.concatenate([right[...]] * 2, axis=0)
    for first in range(0, batch, GROUP):
        for e in range(first, first + GROUP, 2):
            pair = [jnp.concatenate([own[i], other[i]], axis=0) for i in (e, e + 1)]
            sides = jnp.dot(
                factor, jnp.concatenate(pair, axis=1), preferred_element_type=jnp.float32
            )
            for i in range(2):
                term = sides[:, i * width : (i + 1) * width]
                high = term.astype(jnp.bfloat16)
                low = (term - high.astype(jnp.float32)).astype(jnp.bfloat16)
                parts[pl.ds((e - first + i) * side, side), :] = jnp.concatenate(
                    [high, low], axis=1
                )
        product = jnp.dot(parts[...], right_twice, preferred_element_type=jnp.float32)
        full[pl.ds(first * side, GROUP * side), :] = product
        squares = (product * product).reshape(GROUP, side // 8, 8, width)
        sums[pl.ds(first * 8, GROUP * 8), :] = jnp.sum(squares, axis=1).reshape(GROUP * 8, width)
    total = sums[pl.ds(0, batch, stride=8), :]
    for s in range(1, 8):
        total = total + sums[pl.ds(s, batch, stride=8), :]
    mean = jnp.sum(total, axis=1, keepdims=True) / (side * width)
    spread_mean = jnp.broadcast_to(mean, (batch, width))
    step, steps = pl.program_id(0), pl.num_programs(0)
    at = pl.ds(pl.multiple_of(step * batch, batch), batch)
    mean_sq[at] = spread_mean
    scale = lax.rsqrt(spread_mean + 1e-06)
    slices = iter(outs)
    for k in range(quads):
        base = lax.bitwise_xor(here, k) * (half // quads)
        row = 0
        for wide in plan[k]:
            out = next(slices)
            for r in range(wide // width):
                values = full[pl.ds(base + row, batch, stride=side), :]
                out[at, r * width : (r + 1) * width] = (values * scale).astype(jnp.bfloat16)
                row += 1
    if notes:

        @pl.when(step == steps - 1)
        def _():
            every = jnp.concatenate([means_before[...], mean_sq[...]], axis=0)
            means[...] = every
            eye = lax.broadcasted_iota(jnp.int32, (width, width), 0) == lax.broadcasted_iota(
                jnp.int32, (width, width), 1
            )
            lanes = [
                jnp.sum(jnp.where(eye, every[i : i + width], 0.0), axis=0, keepdims=True)
                for i in range(0, every.shape[0], width)
            ]
            term = jnp.concatenate(lanes, axis=1)
            terms = []
            for _ in range(3):
                terms.append(term.astype(jnp.bfloat16).astype(jnp.float32))
                term = term - terms[-1]
            number = lax.broadcasted_iota(jnp.int32, (NOTE, every.shape[0]), 0)
            note = slot_note[...].astype(jnp.float32)
            for i in range(3):
                note = jnp.where(number == 2 + i, terms[i], note)
            slices = iter(outs)
            for k in range(quads):
                out = next(slices)
                rows = out.shape[0] - NOTE
                out[rows:, :] = jnp.zeros((NOTE, out.shape[1]), jnp.bfloat16)
                out[rows:, : every.shape[0]] = note.astype(jnp.bfloat16)
                for _ in plan[k][1:]:
                    next(slices)


def precondition(spot, own, other, left, right, span, plan, slot_note=None, means_before=None):
    _, half, width = own.shape
    side = 2 * half
    first, count, batch = span
    notes = slot_note is not None
    gradient_spec = pl.BlockSpec((batch, half, width), lambda i, s: (first // batch + i, 0, 0))
    whole = lambda shape: pl.BlockSpec(shape, lambda i, s: (0, 0))
    in_specs = [gradient_spec, gradient_spec, whole((side, side)), whole((width, width))]
    operands = [own, other, left, right]
    if notes:
        in_specs += [whole(slot_note.shape), whole(means_before.shape)]
        operands += [slot_note, means_before]
    out_shape = [
        jax.ShapeDtypeStruct((count + (NOTE if notes and f == 0 else 0), wide), jnp.bfloat16)
        for widths in plan
        for f, wide in enumerate(widths)
    ]
    if notes:
        out_shape.append(jax.ShapeDtypeStruct((first + count, width), jnp.float32))
    out_shape.append(jax.ShapeDtypeStruct((count, width), jnp.float32))
    return pl.pallas_call(
        functools.partial(precondition_kernel, plan, notes),
        grid_spec=pltpu.PrefetchScalarGridSpec(
            num_scalar_prefetch=1,
            grid=(count // batch,),
            in_specs=in_specs,
            out_specs=[whole(out.shape) for out in out_shape],
            scratch_shapes=[
                pltpu.VMEM(((batch + 1) * side, width), jnp.float32),
                pltpu.VMEM(((batch + 1) * 8, width), jnp.float32),
                pltpu.VMEM((GROUP * side, 2 * width), jnp.bfloat16),
            ],
        ),
        out_shape=out_shape,
        compiler_params=pltpu.CompilerParams(vmem_limit_bytes=VMEM_BYTES),
        cost_estimate=SMALL_COST,
        name="precondition",
    )(spot, *operands)


def tiles_kernel(order, reach, shapes, based, spot, *rest):
    owners, slots, early_rows, late_rows = shapes
    quads = owners // 2
    block = owners * slots
    notes, inputs = rest[:owners], rest[owners : 3 * owners]
    bases = rest[3 * owners : 3 * owners + 2 * len(PARTS)] if based else ()
    outs, cluster = rest[-2 * len(PARTS) - 1 : -1], rest[-1]
    here, side, core = spot[0], spot[1], spot[2]
    count = early_rows + late_rows
    depth = cluster.shape[3]
    step = pl.program_id(0)

    @pl.when(step == 0)
    def _():
        for source in range(owners):
            note = notes[source][:, :count].astype(jnp.float32).astype(jnp.int32)
            target = note[0:1] + note[1:2] * NOTE_BASE
            slot_of = lax.broadcasted_iota(jnp.int32, (block, count), 0)
            placing = (slot_of == target).astype(jnp.bfloat16)
            early, late = inputs[2 * source : 2 * source + 2]
            values = jnp.concatenate([early[...], late[:late_rows]], axis=0)
            k, m = source % quads, source // quads
            producer = 2 * lax.bitwise_xor(here, k) + lax.bitwise_xor(side, m)
            placed = jnp.dot(placing, values, preferred_element_type=jnp.float32)
            cluster[:, producer] = placed.astype(jnp.bfloat16).reshape(owners, slots, depth)

    half = owners // 2
    rows = half * slots

    @pl.when(step > 0)
    def _():
        k = functools.reduce(lambda v, n: jnp.where(step == n + 1, order[n], v), range(quads), 0)
        owner = 2 * lax.bitwise_xor(here, k) + side
        ahead = [
            cluster[
                lax.rem(owner + j + 1, owners), pl.ds(lax.bitwise_xor(core, h) * half, half)
            ].reshape(rows, depth)
            for h in range(2)
            for j in range(reach)
        ]
        product = lax.dot_general(
            jnp.concatenate(ahead, axis=0),
            cluster[owner].reshape(block, depth),
            (((1,), (1,)), ((), ())),
            preferred_element_type=jnp.float32,
        )
        for h in range(2):
            for n, part in enumerate(PARTS):
                out = h * len(PARTS) + n
                for at, j in enumerate(part):
                    first = (h * reach + j) * rows
                    value = product[first : first + rows]
                    outs[out][0, at] = value + bases[out][0, at] if based else value


def partial_tiles(spot, notes, pieces, width, order, reach, slots, bases=()):
    owners = len(pieces)
    block = owners * slots
    early_rows, late_rows = pieces[0][0][1][1], pieces[0][1][1][1]
    in_specs, operands = [], []
    for array, row in notes:
        in_specs.append(
            pl.BlockSpec((NOTE, 2 * NOTE_BASE), functools.partial(lambda r, i, s: (r, 0), row // NOTE))
        )
        operands.append(array)
    for piece in pieces:
        for array, (row, rows), column in piece:
            if column % width or row % rows:
                array, column, row = array[row : row + rows, column : column + width], 0, 0
            in_specs.append(
                pl.BlockSpec(
                    (rows, width),
                    functools.partial(lambda r, c, i, s: (r, c), row // rows, column // width),
                )
            )
            operands.append(array)
    shapes = [(len(order), len(part), block // 2, block) for part in PARTS] * 2
    tile_specs = [
        pl.BlockSpec((1,) + shape[1:], lambda i, s: (jnp.maximum(i - 1, 0), 0, 0, 0))
        for shape in shapes
    ]
    return pl.pallas_call(
        functools.partial(
            tiles_kernel, order, reach, (owners, slots, early_rows, late_rows), bool(bases)
        ),
        grid_spec=pltpu.PrefetchScalarGridSpec(
            num_scalar_prefetch=1,
            grid=(1 + len(order),),
            in_specs=in_specs + (tile_specs if bases else []),
            out_specs=tile_specs,
            scratch_shapes=[pltpu.VMEM((owners, owners, slots, width), jnp.bfloat16)],
        ),
        out_shape=[jax.ShapeDtypeStruct(shape, jnp.float32) for shape in shapes],
        compiler_params=pltpu.CompilerParams(vmem_limit_bytes=VMEM_BYTES),
        cost_estimate=SMALL_COST,
        name="partial_tiles",
    )(spot, *operands, *bases)


def finish_kernel(spot, flags, *rest):
    *terms, tile, straight, crossed = rest
    total = terms[0][0] + terms[1][0]
    done = (total * flags[0]).astype(tile.dtype)
    tile[...] = done
    turned = done.astype(jnp.float32).T.astype(tile.dtype)
    half = turned.shape[0] // 2
    core = spot[2]
    first, second = turned[:half], turned[half:]
    straight[...] = jnp.where(core == 0, first, second)
    crossed[...] = jnp.where(core == 0, second, first)


def finish(spot, factor, terms, at):
    _, rows, block = terms[0].shape
    spec = lambda shape: pl.BlockSpec(shape, lambda i, s, f: (0, 0))
    out = [(rows, block), (rows, rows), (rows, rows)]
    return pl.pallas_call(
        finish_kernel,
        grid_spec=pltpu.PrefetchScalarGridSpec(
            num_scalar_prefetch=2,
            grid=(1,),
            in_specs=[pl.BlockSpec((1, rows, block), lambda i, s, f: (at, 0, 0))] * 2,
            out_specs=[spec(shape) for shape in out],
        ),
        out_shape=[jax.ShapeDtypeStruct(shape, jnp.bfloat16) for shape in out],
        compiler_params=pltpu.CompilerParams(vmem_limit_bytes=VMEM_BYTES),
        cost_estimate=SMALL_COST,
        name="finish",
    )(spot, factor, *terms)


def split_plan(gradients, owner_of, pair_flags, left_factor, right_factor):
    count, half, width = gradients.shape
    feat = 2 * half * width
    owners = lax.axis_size("blk")
    quads = owners // 2
    reach = pair_flags.shape[1]
    slots = 3 * count // (2 * owners)
    block = owners * slots
    index = lax.axis_index("blk")
    core = lax.axis_index("dim")
    here, side = index // 2, index % 2
    spot = jnp.stack([here, side, core]).astype(jnp.int32)

    def across(x):
        return lax.ppermute(x, "dim", [(0, 1), (1, 0)])

    def along(x, k):
        return lax.ppermute(x, "blk", [(i, i ^ (2 * k)) for i in range(owners)])

    def beside(x):
        return lax.ppermute(x, "blk", [(i, i ^ 1) for i in range(owners)])

    def send(parts):
        return [parts[0]] + [along(parts[k], k) for k in range(1, quads)]

    first = FIRST
    rest_count = count - first
    features = half * width // quads
    widths = [features * n // sum(SLICES) for n in SLICES]
    own_first = gradients[:first]
    other_first = across(own_first)
    (whole,) = after([gradients], other_first)
    other = across(whole)

    *parts, mean_early = precondition(
        spot,
        own_first,
        other_first,
        left_factor,
        right_factor,
        (0, first, first),
        [[features]] * quads,
    )
    *parts, mean_early = after([*parts, mean_early])
    (owner_of,) = after([owner_of], parts[0])
    target = slot_targets(owner_of, owners, slots)
    slot_note = jnp.stack([target % NOTE_BASE, target // NOTE_BASE] + [target] * (NOTE - 2))
    slot_note = slot_note.astype(jnp.bfloat16)
    early = send(parts)
    early.append(beside(early[0]))
    own, *parts, means, _ = precondition(
        spot,
        gradients,
        other,
        left_factor,
        right_factor,
        (first, rest_count, STEP),
        [[features]] + [widths] * (quads - 1),
        slot_note,
        mean_early,
    )
    *early, own = after([*early, own])
    parts = after(parts, own)
    order = [3, 1, 2, 0]
    sums, notes, came = (), [], []
    own_beside = None
    start = 0
    for f in range(len(widths) + 1):
        next_came = []
        if f < len(widths):
            next_came = [along(parts[(k - 1) * len(widths) + f], k) for k in range(1, quads)]
        if f == 0:
            own_beside = beside(own)
            early.append(beside(jnp.concatenate(early[1 : quads - 1], axis=0)))
        if f == 1:
            early.append(beside(early[quads - 1]))
        if f < len(widths):
            crossed = [beside(jnp.concatenate(came, axis=0))] if came else []
        else:
            crossed = [beside(part) for part in came]
        if f >= 2:
            sums = partial_tiles(spot, notes, pieces, widths[f - 2], order, reach, slots, sums)
        every = (next_came, came, crossed, early, own, own_beside, parts, list(sums))
        leaves, structure = jax.tree.flatten(every)
        every = jax.tree.unflatten(structure, after(leaves))
        next_came, came, crossed, early, own, own_beside, parts, sums = every
        if f:
            rows = came[0].shape[0]
            late = [(own, 0)] + [(part, 0) for part in came] + [(own_beside, 0)]
            late += [(crossed[0], rows * k) for k in range(quads - 1)][: len(came) * (f < len(widths))]
            late += [(part, 0) for part in crossed][: len(came) * (f == len(widths))]
            head = [(part, 0) for part in early[: quads + 1]]
            head += [(early[quads + 1], first * k) for k in range(quads - 2)] + [(early[-1], 0)]
            if f == 1:
                notes = [(array, row + rest_count) for array, row in late]
            start = sum(widths[: f - 1])
            pieces = [
                (
                    (head[s][0], (head[s][1], first), start),
                    (late[s][0], (late[s][1], rest_count), 0 if s % quads else start),
                )
                for s in range(owners)
            ]
        came = next_came
    sums = partial_tiles(spot, notes, pieces, widths[-1], order, reach, slots, sums)

    flags = lax.dynamic_index_in_dim(pair_flags, index, 0, keepdims=False).astype(jnp.float32)
    ahead, behind = [None] * reach, [None] * reach
    def back(x, by, turn):
        pairs = [
            (2 * i + c, 2 * ((i + by) % owners) + (1 - c if turn else c))
            for i in range(owners)
            for c in range(2)
        ]
        return lax.ppermute(x, ("blk", "dim"), pairs)

    keeps, gives = sums[: len(PARTS)], sums[len(PARTS) :]
    gots = [across(give) for give in gives]
    odds = [keep[:2] + got[:2] for keep, got in zip(keeps, gots)]
    odds = [along(odd, 1) for odd in odds] + [odds[-1]]
    evens = [[keep[2] + got[2], keep[3] + got[3]] for keep, got in zip(keeps, gots)]
    (odds[0],) = after([odds[0]], odds.pop())
    nears, fars = {}, {}

    def halve(n):
        nears[n] = evens[n][1] + odds[n][1]
        fars[n] = along(evens[n][0] + odds[n][0], 2)

    def complete(n):
        for at, j in enumerate(PARTS[n]):
            factor = (flags[j] * feat ** (-0.5)).reshape(1)
            ahead[j], straight, crossed = finish(spot, factor, [nears[n], fars[n]], at)
            behind[j] = [back(straight, j + 1, False), back(crossed, j + 1, True)]

    last = len(PARTS) - 1
    for n in range(last):
        halve(n)
    complete(0)
    waits = [behind[j][0] for j in PARTS[0]]
    (odds[last],) = after([odds[last]], *waits)
    halve(last)
    for n in range(1, last + 1):
        complete(n)
    for j in range(reach):
        straight, crossed = behind[j]
        behind[j] = jnp.where(
            core == 0,
            jnp.concatenate([straight, crossed], axis=1),
            jnp.concatenate([crossed, straight], axis=1),
        )
    tiles = jnp.stack(ahead + behind).swapaxes(1, 2)

    held = after([array for array, _ in notes], ahead[-1])
    notes = [(array, row) for array, (_, row) in zip(held, notes)]
    note = jnp.stack([array[row : row + 5, :count] for array, row in notes]).astype(jnp.float32)
    targets = note[:, 0:1].astype(jnp.int32) + note[:, 1:2].astype(jnp.int32) * NOTE_BASE
    influences = jnp.log1p(note[:, 2:3] + note[:, 3:4] + note[:, 4:5])
    wanted = index * slots + jnp.arange(slots, dtype=jnp.int32)
    chosen = targets == wanted[None, :, None]
    self_influence = jnp.sum(jnp.where(chosen, influences, 0.0), axis=2)
    self_influence = lax.switch(
        index,
        [
            functools.partial(
                lambda i, x: jnp.stack(
                    [x[(p ^ i) // 2 + (p ^ i) % 2 * quads] for p in range(owners)]
                ).astype(jnp.bfloat16),
                i,
            )
            for i in range(owners)
        ],
        self_influence,
    )
    return (tiles, self_influence.reshape(block))


def solution(mesh):
    owners = mesh.shape["blk"]

    def per_device(gradients, owner_of, pair_flags, left_factor, right_factor):
        block = 3 * gradients.shape[0] // 2
        partial_bytes = 4 * owners * pair_flags.shape[1] * block * block // 2
        quads = owners // 2
        fits = partial_bytes <= PARTIAL_BYTES and quads == 4
        plan = split_plan if fits and (gradients.shape[0] - FIRST) % STEP == 0 and FIRST % STEP == 0 else ring_plan
        return plan(gradients, owner_of, pair_flags, left_factor, right_factor)

    return jax.shard_map(
        per_device,
        mesh=mesh,
        in_specs=(
            P(("groups", "blk"), "dim", None),
            P(("groups", "blk"), None),
            P("groups", None),
            P(),
            P(),
        ),
        out_specs=(P(("groups", "blk"), None, "dim"), P(("groups", "blk"))),
        check_vma=False,
    )
```
